32 devices in a mesh: seq: 16 (over z, y, x), dp: 2 (over core).
Axes of the slice: x: 2, y: 2, z: 4, core: 2. Of those that a mesh axis runs over, the one named last changes fastest.
Arguments:
- query_rows: bfloat16 [2, 2048, 4096], P('dp', 'seq'), may hold values from -6 to 6
- key_rows: bfloat16 [2, 2048, 4096], P('dp', 'seq'), may hold values from -6 to 6
- value_rows: bfloat16 [2, 2048, 4096], P('dp', 'seq'), may hold values from -6 to 6
- cotangent: bfloat16 [2, 2048, 4096], P('dp', 'seq'), may hold values from -6 to 6
- short_filter: float32 [3, 3, 4096], replicated, may hold values from -3 to 3
- residue: float32 [4096, 16], P('seq'), may hold values from -1.5 to 1.5
- decay_rate: float32 [4096, 16], P('seq'), as said below
Outputs:
- query_grad: bfloat16 [2, 2048, 4096], P('dp', 'seq')
- key_grad: bfloat16 [2, 2048, 4096], P('dp', 'seq')
- value_grad: bfloat16 [2, 2048, 4096], P('dp', 'seq')
- short_grad: float32 [3, 3, 4096], replicated
- residue_grad: float32 [4096, 16], P('seq')
- decay_grad: float32 [4096, 16], P('seq')
The draws below stay inside these ranges and needn't reach their ends.
Inputs may be any that keep to these rules, and one draw needn't show every extreme that they name: `decay_rate`: every rate lies between 1 / 20480 and 1 / 32.
All inputs are finite; a program needn't handle non-finite values.
Results may differ from the reference program's by a relative error of at most 0.012.
Values may be sent and summed in bfloat16 or wider, within the bound.
A program may use at most 128 MiB of HBM per device.

```python
import math
import jax
import jax.numpy as jnp
from jax import lax

D = 4096
ORDER = 16
TAPS = 3
SEQLEN = 2048
BATCH = 2


def draw_decay_rate(key, part):
    key = jax.random.fold_in(key, 7)
    first_key, second_key = jax.random.split(key)
    pick = jax.random.uniform(first_key, (D, ORDER), jnp.float32)
    spot = jax.random.uniform(second_key, (D, ORDER), jnp.float32)
    lowest = jnp.log(0.1 / SEQLEN)
    middle = jnp.log(2.0 / SEQLEN)
    highest = jnp.log(1.0 / 32.0)
    share = 0.5
    slower = lowest + spot * (middle - lowest)
    faster = middle + spot * (highest - middle)
    return jnp.exp(jnp.where(pick < share, slower, faster)).astype(jnp.float32)


def shard_levels(own_key, extent, cuts, least, top_value):
    loudness, own = 1.0, jax.random.fold_in(own_key, 6)
    for position, blocks in cuts:
        steps = jnp.exp(jax.random.uniform(jax.random.fold_in(own, position), (blocks,), jnp.float32, least / len(cuts), top_value / len(cuts)))
        loudness = loudness * jnp.repeat(steps, extent[position] // blocks).reshape([-1 if axis == position else 1 for axis in range(len(extent))])
    return loudness


def scatter_about(rng, dims, scale, reach, shards=(), kind=jnp.bfloat16):
    array = jax.random.normal(rng, dims, jnp.float32) * scale
    if len(shards) > 0:
        array = shard_levels(rng, dims, shards, -0.22, 0.18) * array
    return jnp.clip(array, min=-reach, max=reach).astype(kind)


def setup_inputs(seed: int = 0) -> dict:
    splits = jax.random.split(jax.random.key(seed), 8)
    query_rows = scatter_about(splits[0], (BATCH, SEQLEN, D), 1.0, 6.0, ((0, 2), (1, 16)))
    key_rows = scatter_about(splits[1], (BATCH, SEQLEN, D), 1.0, 6.0, ((0, 2), (1, 16)))
    value_rows = scatter_about(splits[2], (BATCH, SEQLEN, D), 1.0, 6.0, ((0, 2), (1, 16)))
    cotangent = scatter_about(splits[3], (BATCH, SEQLEN, D), 1.0, 6.0, ((0, 2), (1, 16)))
    short_filter = scatter_about(splits[4], (3, TAPS, D), 0.5, 3.0, (), jnp.float32)
    residue = scatter_about(splits[5], (D, ORDER), 0.25, 1.5, ((0, 16),), jnp.float32)
    decay_rate = draw_decay_rate(jax.random.fold_in(splits[7], 71), 0)
    return dict(query_rows=query_rows, key_rows=key_rows, value_rows=value_rows, cotangent=cotangent, short_filter=short_filter, residue=residue, decay_rate=decay_rate)


def decay_filter(residue, decay_rate, length):
    times = jnp.arange(length).astype(residue.dtype)
    weights = residue * jnp.sqrt(-jnp.expm1(-2.0 * decay_rate))

    def add_mode(total, pair):
        amount, speed = pair
        return (total + amount[None, :] * jnp.exp(-speed[None, :] * times[:, None]), 0)
    start = jnp.zeros((length, residue.shape[0]), residue.dtype)
    impulse, unused = lax.scan(add_mode, start, (weights.T, decay_rate.T))
    return impulse

def round_trip(values):
    return lax.optimization_barrier(values.astype(jnp.bfloat16)).astype(values.dtype)

def block_pass(query_rows, key_rows, value_rows, cotangent, short_filter, residue, decay_rate):
    batch, length, width = query_rows.shape
    margin = short_filter.shape[1] - 1
    inputs = jnp.stack([query_rows, key_rows, value_rows]).astype(short_filter.dtype)
    padded = jnp.pad(inputs, ((0, 0), (0, 0), (margin, 0), (0, 0)))
    shorted = jnp.zeros_like(inputs)
    for offset in range(margin + 1):
        shorted = shorted + short_filter[:, offset][:, None, None, :] * padded[:, :, margin - offset:margin - offset + length, :]
    query_short, key_short, value_short = (shorted[0], shorted[1], shorted[2])
    gated = round_trip(key_short * value_short)
    impulse, pullback = jax.vjp(lambda amount, speed: decay_filter(amount, speed, length), residue, decay_rate)
    points = 2 * length
    spectrum_u = jnp.fft.rfft(gated, points, axis=1)
    spectrum_h = jnp.fft.rfft(impulse, points, axis=0)[None]
    mixed = round_trip(jnp.fft.irfft(spectrum_u * spectrum_h, points, axis=1)[:, :length])
    upstream = cotangent.astype(short_filter.dtype)
    grad_mixed = round_trip(upstream * query_short)
    spectrum_g = jnp.fft.rfft(grad_mixed, points, axis=1)
    grad_gated = round_trip(jnp.fft.irfft(jnp.conj(spectrum_h) * spectrum_g, points, axis=1)[:, :length])
    grad_impulse = lax.optimization_barrier(jnp.sum(jnp.fft.irfft(spectrum_g * jnp.conj(spectrum_u), points, axis=1)[:, :length], axis=0))
    grad_short = jnp.stack([upstream * mixed, grad_gated * value_short, grad_gated * key_short])
    trailing = jnp.pad(grad_short, ((0, 0), (0, 0), (0, margin), (0, 0)))
    grad_inputs = jnp.zeros_like(grad_short)
    filter_terms = []
    for offset in range(margin + 1):
        grad_inputs = grad_inputs + short_filter[:, offset][:, None, None, :] * trailing[:, :, offset:offset + length, :]
        filter_terms.append(lax.optimization_barrier(jnp.sum(grad_short * padded[:, :, margin - offset:margin - offset + length, :], axis=(1, 2))))
    filter_grad = jnp.stack(filter_terms, axis=1)
    residue_grad, rate_grad = pullback(grad_impulse)
    factor = 1.0 / math.sqrt(batch * length)
    return (grad_inputs[0].astype(jnp.bfloat16), grad_inputs[1].astype(jnp.bfloat16), grad_inputs[2].astype(jnp.bfloat16), filter_grad * factor, residue_grad * factor, decay_rate * rate_grad * factor)

def reference(query_rows, key_rows, value_rows, cotangent, short_filter, residue, decay_rate):
    batch, length, width = query_rows.shape
    block = math.gcd(width, 128)
    count = width // block
    taps = short_filter.shape[1]
    modes = residue.shape[1]

    def to_blocks(values):
        return values.reshape(batch, length, count, block).transpose(2, 0, 1, 3)

    def from_blocks(values):
        return values.transpose(1, 2, 0, 3).reshape(batch, length, width)
    pieces = (to_blocks(query_rows), to_blocks(key_rows), to_blocks(value_rows), to_blocks(cotangent), short_filter.reshape(3, taps, count, block).transpose(2, 0, 1, 3), residue.reshape(count, block, modes), decay_rate.reshape(count, block, modes))

    def one_block(group):
        return block_pass(group[0], group[1], group[2], group[3], group[4], group[5], group[6])
    results = lax.map(one_block, pieces)
    return (from_blocks(results[0]), from_blocks(results[1]), from_blocks(results[2]), results[3].transpose(1, 2, 0, 3).reshape(3, taps, width), results[4].reshape(width, modes), results[5].reshape(width, modes))
```

```python
import functools
import math

import jax
import jax.numpy as jnp
from jax import lax
from jax.experimental import pallas as pl
from jax.experimental.pallas import tpu as pltpu
from jax.sharding import PartitionSpec as P

LANES = 128
GROUPS = 8
WIDE = LANES * GROUPS
F32 = jnp.float32
BF16 = jnp.bfloat16


def row(t):
    start = t * GROUPS
    if not isinstance(t, int):
        start = pl.multiple_of(start, GROUPS)
    return pl.ds(start, GROUPS)


def rounded(values):
    return values.astype(BF16).astype(F32)


def spread_rows(source, target, shift, tokens):
    def step(i, carry):
        start = pl.multiple_of(i * 16, 16)
        for s in range(GROUPS):
            piece = source[0, pl.ds(start, 16), s * LANES : (s + 1) * LANES].astype(F32)
            target[pl.ds((start + shift) * GROUPS + s, 16, stride=GROUPS), :] = piece
        return carry

    lax.fori_loop(0, tokens // 16, step, 0)


def gather_rows(source, target, tokens):
    def step(i, carry):
        start = pl.multiple_of(i * 16, 16)
        for s in range(GROUPS):
            piece = source[pl.ds(start * GROUPS + s, 16, stride=GROUPS), :]
            target[0, pl.ds(start, 16), s * LANES : (s + 1) * LANES] = piece.astype(BF16)
        return carry

    lax.fori_loop(0, tokens // 16, step, 0)


def load_inputs(tokens, margin, rows, before, after, wide):
    for i in range(4):
        spread_rows(rows[i], wide[i], margin, tokens)
        for j in range(margin):
            if i < 3:
                wide[i][row(j), :] = before[i, j].astype(F32)
            wide[i][row(margin + tokens + j), :] = after[i, j].astype(F32)


def short_products(tokens, margin, taps, wide, gated, grad_mixed, keep):
    weights = [[taps[i, j] for j in range(margin + 1)] for i in range(3)]

    def step(t, carry):
        shorted = []
        for i in range(3):
            total = weights[i][0] * wide[i][row(t + margin), :]
            for j in range(1, margin + 1):
                total = total + weights[i][j] * wide[i][row(t + margin - j), :]
            shorted.append(total)
        gated[row(t), :] = rounded(shorted[1] * shorted[2])
        grad_mixed[row(t), :] = rounded(wide[3][row(t + margin), :] * shorted[0])
        if keep is not None:
            keep[0][row(t), :] = shorted[1]
            keep[1][row(t), :] = shorted[2]
        return carry

    lax.fori_loop(0, tokens + margin, step, 0, unroll=2)


def ends_kernel(tokens, margin, modes, q, k, v, c, before, after, taps, rate, state, w0, w1, w2, w3, gated, grad_mixed):
    wide = (w0, w1, w2, w3)
    load_inputs(tokens, margin, (q, k, v, c), before, after, wide)
    short_products(tokens, margin, taps, wide, gated, grad_mixed, None)
    decay = [jnp.exp(-rate[n]) for n in range(modes)]
    zero = jnp.zeros((GROUPS, LANES), F32)

    def step(t, carry):
        ahead, back = carry
        u = gated[row(t), :]
        g = grad_mixed[row(tokens - 1 - t), :]
        return (
            tuple(decay[n] * ahead[n] + u for n in range(modes)),
            tuple(decay[n] * back[n] + g for n in range(modes)),
        )

    ahead, back = lax.fori_loop(0, tokens, step, ((zero,) * modes, (zero,) * modes), unroll=2)
    for n in range(modes):
        state[n, 0, 0] = ahead[n]
        state[n, 0, 1] = back[n]


def main_kernel(
    tokens, margin, modes, part, q, k, v, c, before, after, taps, rate, weight, state,
    dq, dk, dv, sums, tap_sums,
    w0, w1, w2, w3, gated, grad_mixed, keys, values, mixed, grad_gated, trail, o0, o1, o2,
):
    wide = (w0, w1, w2, w3)
    load_inputs(tokens, margin, (q, k, v, c), before, after, wide)
    short_products(tokens, margin, taps, wide, gated, grad_mixed, (keys, values))
    zero = jnp.zeros((GROUPS, LANES), F32)
    for first in range(0, modes, part):
        some = range(first, first + part)
        decay = [jnp.exp(-rate[n]) for n in some]
        amount = [weight[n] for n in some]

        def total_of(terms):
            terms = list(terms)
            while len(terms) > 1:
                terms = [a + b for a, b in zip(terms[::2], terms[1::2])]
            return terms[0]

        def forward(t, carry):
            x, dots = carry
            u = gated[row(t), :]
            g = grad_mixed[row(t), :]
            x = tuple(decay[n] * x[n] + u for n in range(part))
            for n in range(part):
                trail[row(t * part + n), :] = x[n]
            y = total_of(amount[n] * x[n] for n in range(part))
            if first > 0:
                y = y + mixed[row(t), :]
            mixed[row(t), :] = y
            return (x, tuple(dots[n] + g * x[n] for n in range(part)))

        start = tuple(state[n, 0, 0] for n in some)
        x, dots = lax.fori_loop(0, tokens, forward, (start, (zero,) * part), unroll=2)
        for n in range(part):
            sums[0, first + n] = dots[n]
        for t in range(tokens, tokens + margin):
            u = gated[row(t), :]
            x = tuple(decay[n] * x[n] + u for n in range(part))
            y = total_of(amount[n] * x[n] for n in range(part))
            if first > 0:
                y = y + mixed[row(t), :]
            mixed[row(t), :] = y

        def backward(i, carry):
            t = tokens - 1 - i
            h, dots = carry
            g = grad_mixed[row(t), :]
            dots = tuple(dots[n] + trail[row(t * part + n), :] * h[n] for n in range(part))
            h = tuple(decay[n] * h[n] + g for n in range(part))
            y = total_of(amount[n] * h[n] for n in range(part))
            if first > 0:
                y = y + grad_gated[row(t), :]
            grad_gated[row(t), :] = y
            return (h, dots)

        start = tuple(state[n, 0, 1] for n in some)
        h, dots = lax.fori_loop(0, tokens, backward, (start, (zero,) * part), unroll=2)
        for n in range(part):
            sums[1, first + n] = decay[n] * dots[n]
        grow = [jnp.exp(rate[n]) for n in some]
        h = start
        for t in range(tokens, tokens + margin):
            y = total_of(amount[n] * h[n] for n in range(part))
            if first > 0:
                y = y + grad_gated[row(t), :]
            grad_gated[row(t), :] = y
            g = grad_mixed[row(t), :]
            h = tuple((h[n] - g) * grow[n] for n in range(part))

    filters = [[taps[i, j] for j in range(margin + 1)] for i in range(3)]
    outs = (o0, o1, o2)

    def grads_at(t):
        m = rounded(mixed[row(t), :])
        gg = rounded(grad_gated[row(t), :])
        return (wide[3][row(t + margin), :] * m, gg * values[row(t), :], gg * keys[row(t), :])

    def finish(i, carry):
        t = tokens - 1 - i
        later, dots = carry
        now = grads_at(t)
        window = (now,) + later
        new = []
        for a in range(3):
            total = filters[a][0] * now[a]
            for j in range(1, margin + 1):
                total = total + filters[a][j] * window[j][a]
            outs[a][row(t), :] = total
            for j in range(margin + 1):
                new.append(dots[a * (margin + 1) + j] + now[a] * wide[a][row(t + margin - j), :])
        return (window[:margin], tuple(new))

    later = tuple(grads_at(tokens + j) for j in range(margin))
    later, dots = lax.fori_loop(0, tokens, finish, (later, (zero,) * (3 * (margin + 1))), unroll=2)
    for a in range(3):
        for j in range(margin + 1):
            tap_sums[a, j] = dots[a * (margin + 1) + j]
    for source, target in zip(outs, (dq, dk, dv)):
        gather_rows(source, target, tokens)


def carry_kernel(count, power, got, out):
    factor = power[...]
    ahead = jnp.zeros_like(factor)
    back = jnp.zeros_like(factor)
    for p in range(count):
        out[p, 0] = ahead
        ahead = factor * ahead + got[p, 0]
        out[count - 1 - p, 1] = back
        back = factor * back + got[count - 1 - p, 1]


def swap(blocks):
    return lax.all_to_all(blocks, "seq", split_axis=0, concat_axis=0, tiled=True)


def passed_along(shard, axis, by):
    count = lax.axis_size(axis)
    pairs = [(i, i + by) for i in range(count) if 0 <= i + by < count]
    return lax.ppermute(shard, axis, pairs)


def body(query_rows, key_rows, value_rows, cotangent, short_filter, residue, decay_rate):
    batch, tokens, width = query_rows.shape
    assert batch == 1
    margin = short_filter.shape[1] - 1
    modes = residue.shape[1]
    count = lax.axis_size("seq")
    own = residue.shape[0] // LANES
    tiles = width // LANES
    split = count // modes
    assert split * modes == count
    per = tiles // split // GROUPS
    blocks = width // WIDE
    length = tokens * count
    vmem = 56 << 20

    root = jnp.sqrt(-jnp.expm1(-2.0 * decay_rate))
    mine = jnp.stack([decay_rate.T, (residue * root).T]).reshape(2, modes, own, LANES)
    everyone = lax.all_gather(mine, "seq")
    rate, weight = everyone.transpose(1, 2, 0, 3, 4).reshape(2, modes, tiles, LANES)

    rows = (query_rows, key_rows, value_rows, cotangent)
    before = jnp.stack([x[0, tokens - margin :] for x in rows[:3]])
    before = passed_along(before, "seq", 1).reshape(3, margin, tiles, LANES)
    after = jnp.stack([x[0, :margin] for x in rows])
    after = passed_along(after, "seq", -1).reshape(4, margin, tiles, LANES)
    taps = short_filter.reshape(3, margin + 1, tiles, LANES)

    rows_spec = pl.BlockSpec((1, tokens, WIDE), lambda i: (0, 0, i))

    def tile_spec(*lead):
        zeros = (0,) * len(lead)
        return pl.BlockSpec(lead + (GROUPS, LANES), lambda i: zeros + (i, 0))

    state_spec = pl.BlockSpec(
        (modes, 1, 2, GROUPS, LANES), lambda i: (0, i // per, 0, i % per, 0)
    )

    def scratch(n):
        return pltpu.VMEM((n * GROUPS, LANES), F32)

    params = pltpu.CompilerParams(vmem_limit_bytes=vmem)
    head = [rows_spec] * 4 + [tile_spec(3, margin), tile_spec(4, margin), tile_spec(3, margin + 1), tile_spec(modes)]
    wide = [scratch(tokens + 2 * margin)] * 4
    state = pl.pallas_call(
        functools.partial(ends_kernel, tokens, margin, modes),
        grid=(blocks,),
        in_specs=head,
        out_specs=state_spec,
        out_shape=jax.ShapeDtypeStruct((modes, split, 2, tiles // split, LANES), F32),
        scratch_shapes=wide + [scratch(tokens + margin)] * 2,
        compiler_params=params,
        name="block_ends",
    )(*rows, before, after, taps, rate)

    got = swap(state.reshape(count, 2, tiles // split, LANES))
    slices = rate.reshape(count, tiles // split, LANES)
    power = jnp.exp(-tokens * lax.dynamic_index_in_dim(slices, lax.axis_index("seq"), 0, False))
    carried = pl.pallas_call(
        functools.partial(carry_kernel, count),
        out_shape=jax.ShapeDtypeStruct(got.shape, F32),
        name="carries",
    )(power, got)
    state = swap(carried).reshape(state.shape)

    shapes = [jax.ShapeDtypeStruct(query_rows.shape, BF16)] * 3
    dq, dk, dv, sums, tap_sums = pl.pallas_call(
        functools.partial(main_kernel, tokens, margin, modes, modes // 2),
        grid=(blocks,),
        in_specs=head + [tile_spec(modes), state_spec],
        out_specs=[rows_spec] * 3 + [tile_spec(2, modes), tile_spec(3, margin + 1)],
        out_shape=shapes
        + [
            jax.ShapeDtypeStruct((2, modes, tiles, LANES), F32),
            jax.ShapeDtypeStruct((3, margin + 1, tiles, LANES), F32),
        ],
        scratch_shapes=wide
        + [scratch(tokens + margin)] * 6
        + [scratch(tokens * modes // 2)]
        + [scratch(tokens)] * 3,
        compiler_params=params,
        name="mixer",
    )(*rows, before, after, taps, rate, weight, state)

    terms = 2 * modes + 3 * (margin + 1)
    packed = jnp.concatenate(
        [sums.reshape(2 * modes, count, own, LANES), tap_sums.reshape(-1, count, own, LANES)]
    ).transpose(1, 0, 2, 3)
    reduced = lax.psum(jnp.sum(swap(packed), axis=0), "dp")
    factor = 1.0 / math.sqrt(batch * lax.axis_size("dp") * length)
    reduced = reduced * factor
    filter_grad = lax.all_gather(reduced[2 * modes :], "seq", axis=1)
    filter_grad = filter_grad.reshape(3, margin + 1, width)
    first_sum, second_sum = (
        reduced[: 2 * modes].reshape(2, modes, own * LANES).transpose(0, 2, 1)
    )
    residue_grad = root * first_sum
    rate_grad = (
        residue * jnp.exp(-2.0 * decay_rate) / root * first_sum - residue * root * second_sum
    )
    return (dq, dk, dv, filter_grad, residue_grad, decay_rate * rate_grad)


def solution(mesh):
    rows = P("dp", "seq", None)
    modes = P("seq", None)
    return jax.shard_map(
        body,
        mesh=mesh,
        in_specs=(rows, rows, rows, rows, P(), modes, modes),
        out_specs=(rows, rows, rows, P(), modes, modes),
        check_vma=False,
    )
```

```python
import functools
import math

import jax
import jax.numpy as jnp
from jax import lax
from jax.experimental import pallas as pl
from jax.experimental.pallas import tpu as pltpu
from jax.sharding import PartitionSpec as P

LANES = 128
GROUPS = 8
WIDE = LANES * GROUPS
F32 = jnp.float32
BF16 = jnp.bfloat16


def row(t):
    start = t * GROUPS
    if not isinstance(t, int):
        start = pl.multiple_of(start, GROUPS)
    return pl.ds(start, GROUPS)


def rounded(values):
    return values.astype(BF16).astype(F32)


def spread_rows(source, target, shift, tokens):
    def step(i, carry):
        start = pl.multiple_of(i * 16, 16)
        for s in range(GROUPS):
            piece = source[0, pl.ds(start, 16), s * LANES : (s + 1) * LANES].astype(F32)
            target[pl.ds((start + shift) * GROUPS + s, 16, stride=GROUPS), :] = piece
        return carry

    lax.fori_loop(0, tokens // 16, step, 0)


def gather_rows(source, target, tokens):
    def step(i, carry):
        start = pl.multiple_of(i * 16, 16)
        for s in range(GROUPS):
            piece = source[pl.ds(start * GROUPS + s, 16, stride=GROUPS), :]
            target[0, pl.ds(start, 16), s * LANES : (s + 1) * LANES] = piece.astype(BF16)
        return carry

    lax.fori_loop(0, tokens // 16, step, 0)


def load_inputs(tokens, margin, rows, before, after, wide):
    for i in range(4):
        spread_rows(rows[i], wide[i], margin, tokens)
        for j in range(margin):
            if i < 3:
                wide[i][row(j), :] = before[i, j].astype(F32)
            wide[i][row(margin + tokens + j), :] = after[i, j].astype(F32)


def short_products(tokens, margin, taps, wide, gated, grad_mixed, keep):
    weights = [[taps[i, j] for j in range(margin + 1)] for i in range(3)]

    def step(t, carry):
        shorted = []
        for i in range(3):
            total = weights[i][0] * wide[i][row(t + margin), :]
            for j in range(1, margin + 1):
                total = total + weights[i][j] * wide[i][row(t + margin - j), :]
            shorted.append(total)
        gated[row(t), :] = rounded(shorted[1] * shorted[2])
        grad_mixed[row(t), :] = rounded(wide[3][row(t + margin), :] * shorted[0])
        if keep is not None:
            keep[0][row(t), :] = shorted[1]
            keep[1][row(t), :] = shorted[2]
        return carry

    lax.fori_loop(0, tokens + margin, step, 0, unroll=2)


def ends_kernel(tokens, margin, modes, q, k, v, c, before, after, taps, rate, state, w0, w1, w2, w3, gated, grad_mixed):
    wide = (w0, w1, w2, w3)
    load_inputs(tokens, margin, (q, k, v, c), before, after, wide)
    short_products(tokens, margin, taps, wide, gated, grad_mixed, None)
    decay = [jnp.exp(-rate[n]) for n in range(modes)]
    zero = jnp.zeros((GROUPS, LANES), F32)

    def step(t, carry):
        ahead, back = carry
        u = gated[row(t), :]
        g = grad_mixed[row(tokens - 1 - t), :]
        return (
            tuple(decay[n] * ahead[n] + u for n in range(modes)),
            tuple(decay[n] * back[n] + g for n in range(modes)),
        )

    ahead, back = lax.fori_loop(0, tokens, step, ((zero,) * modes, (zero,) * modes), unroll=2)
    for n in range(modes):
        state[n, 0, 0] = ahead[n]
        state[n, 0, 1] = back[n]


def main_kernel(
    tokens, margin, modes, part, q, k, v, c, before, after, taps, rate, weight, state,
    dq, dk, dv, sums, tap_sums,
    w0, w1, w2, w3, gated, grad_mixed, keys, values, mixed, grad_gated, trail, o0, o1, o2,
):
    wide = (w0, w1, w2, w3)
    load_inputs(tokens, margin, (q, k, v, c), before, after, wide)
    short_products(tokens, margin, taps, wide, gated, grad_mixed, (keys, values))
    zero = jnp.zeros((GROUPS, LANES), F32)
    for first in range(0, modes, part):
        some = range(first, first + part)
        decay = [jnp.exp(-rate[n]) for n in some]
        amount = [weight[n] for n in some]

        def total_of(terms):
            terms = list(terms)
            while len(terms) > 1:
                terms = [a + b for a, b in zip(terms[::2], terms[1::2])]
            return terms[0]

        def forward(t, carry):
            x, dots = carry
            u = gated[row(t), :]
            g = grad_mixed[row(t), :]
            x = tuple(decay[n] * x[n] + u for n in range(part))
            for n in range(part):
                trail[row(t * part + n), :] = x[n]
            y = total_of(amount[n] * x[n] for n in range(part))
            if first > 0:
                y = y + mixed[row(t), :]
            mixed[row(t), :] = y
            return (x, tuple(dots[n] + g * x[n] for n in range(part)))

        start = tuple(state[n, 0, 0] for n in some)
        x, dots = lax.fori_loop(0, tokens, forward, (start, (zero,) * part), unroll=2)
        for n in range(part):
            sums[0, first + n] = dots[n]
        for t in range(tokens, tokens + margin):
            u = gated[row(t), :]
            x = tuple(decay[n] * x[n] + u for n in range(part))
            y = total_of(amount[n] * x[n] for n in range(part))
            if first > 0:
                y = y + mixed[row(t), :]
            mixed[row(t), :] = y

        def backward(i, carry):
            t = tokens - 1 - i
            h, dots = carry
            g = grad_mixed[row(t), :]
            dots = tuple(dots[n] + trail[row(t * part + n), :] * h[n] for n in range(part))
            h = tuple(decay[n] * h[n] + g for n in range(part))
            y = total_of(amount[n] * h[n] for n in range(part))
            if first > 0:
                y = y + grad_gated[row(t), :]
            grad_gated[row(t), :] = y
            return (h, dots)

        start = tuple(state[n, 0, 1] for n in some)
        h, dots = lax.fori_loop(0, tokens, backward, (start, (zero,) * part), unroll=2)
        for n in range(part):
            sums[1, first + n] = decay[n] * dots[n]
        grow = [jnp.exp(rate[n]) for n in some]
        h = start
        for t in range(tokens, tokens + margin):
            y = total_of(amount[n] * h[n] for n in range(part))
            if first > 0:
                y = y + grad_gated[row(t), :]
            grad_gated[row(t), :] = y
            g = grad_mixed[row(t), :]
            h = tuple((h[n] - g) * grow[n] for n in range(part))

    filters = [[taps[i, j] for j in range(margin + 1)] for i in range(3)]
    outs = (o0, o1, o2)

    def grads_at(t):
        m = rounded(mixed[row(t), :])
        gg = rounded(grad_gated[row(t), :])
        return (wide[3][row(t + margin), :] * m, gg * values[row(t), :], gg * keys[row(t), :])

    def finish(i, carry):
        t = tokens - 1 - i
        later, dots = carry
        now = grads_at(t)
        window = (now,) + later
        new = []
        for a in range(3):
            total = filters[a][0] * now[a]
            for j in range(1, margin + 1):
                total = total + filters[a][j] * window[j][a]
            outs[a][row(t), :] = total
            for j in range(margin + 1):
                new.append(dots[a * (margin + 1) + j] + now[a] * wide[a][row(t + margin - j), :])
        return (window[:margin], tuple(new))

    later = tuple(grads_at(tokens + j) for j in range(margin))
    later, dots = lax.fori_loop(0, tokens, finish, (later, (zero,) * (3 * (margin + 1))), unroll=2)
    for a in range(3):
        for j in range(margin + 1):
            tap_sums[a, j] = dots[a * (margin + 1) + j]
    for source, target in zip(outs, (dq, dk, dv)):
        gather_rows(source, target, tokens)


MESH = pl.DeviceIdType.MESH


def partner(d):
    count = lax.axis_size("seq")
    return lax.rem(lax.axis_index("seq") + d, count)


def core_of():
    return lax.rem(lax.axis_index("dp"), 2)


def other_core():
    return lax.axis_index("dp") + 1 - 2 * core_of()


def greet():
    count = lax.axis_size("seq")
    barrier = pltpu.get_barrier_semaphore()
    for d in range(1, count):
        pl.semaphore_signal(barrier, inc=1, device_id={"seq": partner(d)}, device_id_type=MESH)
    pl.semaphore_signal(barrier, inc=1, device_id={"dp": other_core()}, device_id_type=MESH)
    pl.semaphore_wait(barrier, count)


def remote(source, target, sems, d, device):
    return pltpu.make_async_remote_copy(
        src_ref=source,
        dst_ref=target,
        send_sem=sems.at[0, d],
        recv_sem=sems.at[1, d],
        device_id=device,
        device_id_type=MESH,
    )


def to_all(source_of, target, sems):
    me = lax.axis_index("seq")
    copies = []
    for d in range(1, lax.axis_size("seq")):
        copy = remote(source_of(partner(d)), target.at[me], sems, d, {"seq": partner(d)})
        copy.start()
        copies.append(copy)
    return copies


def wait_all(copies):
    for copy in copies:
        copy.wait()


def start_kernel(
    mine, before, after, everyone, got_before, got_after, slots, left, right, sems, halo_sems, swap_sems
):
    me = lax.axis_index("seq")
    count = lax.axis_size("seq")
    core = core_of()
    greet()
    halos = [
        remote(before, left, halo_sems, 0, {"seq": partner(1)}),
        remote(after, right, halo_sems, 1, {"seq": partner(count - 1)}),
    ]
    for copy in halos:
        copy.start()
    copies = to_all(lambda p: mine.at[core], slots.at[core], sems)
    slots[core, me] = mine[core]
    wait_all(copies)
    copy = remote(slots.at[core], slots.at[core], swap_sems, 0, {"dp": other_core()})
    copy.start()
    wait_all(halos)
    got_before[...] = jnp.where(me > 0, left[...].astype(F32), 0.0).astype(BF16)
    got_after[...] = jnp.where(me < count - 1, right[...].astype(F32), 0.0).astype(BF16)
    copy.wait()
    everyone[...] = slots[...]


def carry_kernel(state, power, out, got, sent, landed, out_sems, back_sems):
    me = lax.axis_index("seq")
    count = lax.axis_size("seq")
    greet()
    copies = to_all(lambda p: state.at[p], got, out_sems)
    got[me] = state[me]
    factor = power[...]
    ahead = jnp.zeros_like(factor)
    back = jnp.zeros_like(factor)
    wait_all(copies)
    for p in range(count):
        sent[p, 0] = ahead
        ahead = factor * ahead + got[p, 0]
        sent[count - 1 - p, 1] = back
        back = factor * back + got[count - 1 - p, 1]
    copies = to_all(lambda p: sent.at[p], landed, back_sems)
    landed[me] = sent[me]
    wait_all(copies)
    out[...] = landed[...]


def reduce_kernel(packed, out, other, summed, got, sems, swap_sems):
    me = lax.axis_index("seq")
    core = core_of()
    greet()
    copy = remote(packed.at[1 - core], other, swap_sems, 0, {"dp": other_core()})
    copy.start()
    copy.wait()
    summed[...] = packed[core] + other[...]
    copies = to_all(lambda p: summed.at[p], got, sems)
    got[me] = summed[me]
    wait_all(copies)
    total = got[0]
    for p in range(1, got.shape[0]):
        total = total + got[p]
    out[...] = total


def share_kernel(start, half, out, taps, both, slots, sems, swap_sems):
    me = lax.axis_index("seq")
    core = core_of()
    greet()
    both[core] = half[...]
    copy = remote(both.at[core], both.at[core], swap_sems, 0, {"dp": other_core()})
    copy.start()
    copy.wait()
    rows = both.at[1, pl.ds(start, slots.shape[1])]
    copies = to_all(lambda p: rows, slots, sems)
    slots[me] = both[1, pl.ds(start, slots.shape[1])]
    wait_all(copies)
    out[...] = both[...]
    taps[...] = slots[...]


def comm_call(kernel, ident, name, shapes, scratch):
    return pl.pallas_call(
        kernel,
        out_shape=shapes,
        scratch_shapes=scratch,
        compiler_params=pltpu.CompilerParams(
            collective_id=ident, has_side_effects=True, vmem_limit_bytes=32 << 20
        ),
        name=name,
    )


def body(query_rows, key_rows, value_rows, cotangent, short_filter, residue, decay_rate):
    batch, tokens, width = query_rows.shape
    assert batch == 1
    margin = short_filter.shape[1] - 1
    modes = residue.shape[1]
    count = lax.axis_size("seq")
    own = residue.shape[0] // LANES
    tiles = width // LANES
    split = count // modes
    assert split * modes == count
    per = tiles // split // GROUPS
    blocks = width // WIDE
    length = tokens * count
    vmem = 56 << 20

    root = jnp.sqrt(-jnp.expm1(-2.0 * decay_rate))
    both = pltpu.SemaphoreType.DMA((2, count))
    pair = pltpu.SemaphoreType.DMA((2, 2))
    mine = jnp.stack([decay_rate.T, (residue * root).T]).reshape(2, modes * own, LANES)
    rows = (query_rows, key_rows, value_rows, cotangent)
    before = jnp.stack([x[0, tokens - margin :] for x in rows[:3]])
    before = before.reshape(3, margin, tiles, LANES)
    after = jnp.stack([x[0, :margin] for x in rows]).reshape(4, margin, tiles, LANES)
    slots = (2, count, modes * own, LANES)
    everyone, before, after = comm_call(
        start_kernel,
        0,
        "gather_modes",
        [
            jax.ShapeDtypeStruct(slots, F32),
            jax.ShapeDtypeStruct(before.shape, BF16),
            jax.ShapeDtypeStruct(after.shape, BF16),
        ],
        [
            pltpu.VMEM(slots, F32),
            pltpu.VMEM(before.shape, BF16),
            pltpu.VMEM(after.shape, BF16),
            both,
            pair,
            pair,
        ],
    )(mine, before, after)
    everyone = everyone.reshape(2, count, modes, own, LANES)
    rate, weight = everyone.transpose(0, 2, 1, 3, 4).reshape(2, modes, tiles, LANES)
    taps = short_filter.reshape(3, margin + 1, tiles, LANES)

    rows_spec = pl.BlockSpec((1, tokens, WIDE), lambda i: (0, 0, i))

    def tile_spec(*lead):
        zeros = (0,) * len(lead)
        return pl.BlockSpec(lead + (GROUPS, LANES), lambda i: zeros + (i, 0))

    state_spec = pl.BlockSpec(
        (modes, 1, 2, GROUPS, LANES), lambda i: (0, i // per, 0, i % per, 0)
    )

    def scratch(n):
        return pltpu.VMEM((n * GROUPS, LANES), F32)

    params = pltpu.CompilerParams(vmem_limit_bytes=vmem)
    head = [rows_spec] * 4 + [tile_spec(3, margin), tile_spec(4, margin), tile_spec(3, margin + 1), tile_spec(modes)]
    wide = [scratch(tokens + 2 * margin)] * 4
    state = pl.pallas_call(
        functools.partial(ends_kernel, tokens, margin, modes),
        grid=(blocks,),
        in_specs=head,
        out_specs=state_spec,
        out_shape=jax.ShapeDtypeStruct((modes, split, 2, tiles // split, LANES), F32),
        scratch_shapes=wide + [scratch(tokens + margin)] * 2,
        compiler_params=params,
        name="block_ends",
    )(*rows, before, after, taps, rate)

    slices = rate.reshape(count, tiles // split, LANES)
    power = jnp.exp(-tokens * lax.dynamic_index_in_dim(slices, lax.axis_index("seq"), 0, False))
    blocked = (count, 2, tiles // split, LANES)
    state = comm_call(
        carry_kernel,
        1,
        "carry_states",
        jax.ShapeDtypeStruct(blocked, F32),
        [pltpu.VMEM(blocked, F32)] * 3 + [both] * 2,
    )(state.reshape(blocked), power).reshape(state.shape)

    shapes = [jax.ShapeDtypeStruct(query_rows.shape, BF16)] * 3
    dq, dk, dv, sums, tap_sums = pl.pallas_call(
        functools.partial(main_kernel, tokens, margin, modes, modes // 2),
        grid=(blocks,),
        in_specs=head + [tile_spec(modes), state_spec],
        out_specs=[rows_spec] * 3 + [tile_spec(2, modes), tile_spec(3, margin + 1)],
        out_shape=shapes
        + [
            jax.ShapeDtypeStruct((2, modes, tiles, LANES), F32),
            jax.ShapeDtypeStruct((3, margin + 1, tiles, LANES), F32),
        ],
        scratch_shapes=wide
        + [scratch(tokens + margin)] * 6
        + [scratch(tokens * modes // 2)]
        + [scratch(tokens)] * 3,
        compiler_params=params,
        name="mixer",
    )(*rows, before, after, taps, rate, weight, state)

    terms = (2 * modes + 3 * (margin + 1)) * own
    sum_rows = 2 * modes * own
    padded = -(-terms // 16) * 16
    half = padded // 2
    packed = jnp.concatenate(
        [sums.reshape(2 * modes, count, own, LANES), tap_sums.reshape(-1, count, own, LANES)]
    )
    packed = packed.transpose(1, 0, 2, 3).reshape(count, terms, LANES)
    packed = jnp.pad(packed, ((0, 0), (0, padded - terms), (0, 0)))
    packed = packed.reshape(count, 2, half, LANES).transpose(1, 0, 2, 3)
    blocked = (count, half, LANES)
    reduced = comm_call(
        reduce_kernel,
        2,
        "reduce_sums",
        jax.ShapeDtypeStruct((half, LANES), F32),
        [pltpu.VMEM(blocked, F32)] * 3 + [both, pair],
    )(packed)
    cores = lax.axis_size("dp")
    if cores > 2:
        groups = [[j for j in range(cores) if j % 2 == i] for i in range(2)]
        reduced = lax.psum(reduced, "dp", axis_index_groups=groups)
    tap_start = sum_rows - half
    tap_rows = padded - sum_rows
    slots = (count, tap_rows, LANES)
    reduced, filter_grad = comm_call(
        functools.partial(share_kernel, tap_start),
        3,
        "share_taps",
        [jax.ShapeDtypeStruct((2, half, LANES), F32), jax.ShapeDtypeStruct(slots, F32)],
        [pltpu.VMEM((2, half, LANES), F32), pltpu.VMEM(slots, F32), both, pair],
    )(reduced)
    factor = 1.0 / math.sqrt(batch * cores * length)
    reduced = reduced.reshape(padded, LANES)[:sum_rows] * factor
    filter_grad = filter_grad[:, : terms - sum_rows] * factor
    filter_grad = filter_grad.reshape(count, 3, margin + 1, own * LANES).transpose(1, 2, 0, 3)
    filter_grad = filter_grad.reshape(3, margin + 1, width)
    first_sum, second_sum = (
        reduced.reshape(2, modes, own * LANES).transpose(0, 2, 1)
    )
    residue_grad = root * first_sum
    rate_grad = (
        residue * jnp.exp(-2.0 * decay_rate) / root * first_sum - residue * root * second_sum
    )
    return (dq, dk, dv, filter_grad, residue_grad, decay_rate * rate_grad)


def solution(mesh):
    rows = P("dp", "seq", None)
    modes = P("seq", None)
    return jax.shard_map(
        body,
        mesh=mesh,
        in_specs=(rows, rows, rows, rows, P(), modes, modes),
        out_specs=(rows, rows, rows, P(), modes, modes),
        check_vma=False,
    )
```

```python
import functools
import math

import jax
import jax.numpy as jnp
from jax import lax
from jax.experimental import pallas as pl
from jax.experimental.pallas import tpu as pltpu
from jax.sharding import PartitionSpec as P

LANES = 128
GROUPS = 8
WIDE = LANES * GROUPS
F32 = jnp.float32
BF16 = jnp.bfloat16


def row(t):
    start = t * GROUPS
    if not isinstance(t, int):
        start = pl.multiple_of(start, GROUPS)
    return pl.ds(start, GROUPS)


def rounded(values):
    return values.astype(BF16).astype(F32)


def spread_rows(source, target, shift, tokens, base=0):
    def step(i, carry):
        start = pl.multiple_of(i * 16, 16)
        for s in range(GROUPS):
            piece = source[0, pl.ds(start, 16), pl.ds(base + s * LANES, LANES)].astype(F32)
            target[pl.ds((start + shift) * GROUPS + s, 16, stride=GROUPS), :] = piece
        return carry

    lax.fori_loop(0, tokens // 16, step, 0)


def gather_rows(source, target, tokens):
    def step(i, carry):
        start = pl.multiple_of(i * 16, 16)
        for s in range(GROUPS):
            piece = source[pl.ds(start * GROUPS + s, 16, stride=GROUPS), :]
            target[0, pl.ds(start, 16), s * LANES : (s + 1) * LANES] = piece.astype(BF16)
        return carry

    lax.fori_loop(0, tokens // 16, step, 0)


def load_inputs(tokens, margin, rows, before, after, wide):
    for i in range(4):
        spread_rows(rows[i], wide[i], margin, tokens)
        for j in range(margin):
            if i < 3:
                wide[i][row(j), :] = before[i, j].astype(F32)
            wide[i][row(margin + tokens + j), :] = after[i, j].astype(F32)


def short_products(tokens, margin, taps, wide, gated, grad_mixed, keep):
    weights = [[taps[i, j] for j in range(margin + 1)] for i in range(3)]

    def step(t, carry):
        shorted = []
        for i in range(3):
            total = weights[i][0] * wide[i][row(t + margin), :]
            for j in range(1, margin + 1):
                total = total + weights[i][j] * wide[i][row(t + margin - j), :]
            shorted.append(total)
        gated[row(t), :] = rounded(shorted[1] * shorted[2])
        grad_mixed[row(t), :] = rounded(wide[3][row(t + margin), :] * shorted[0])
        if keep is not None:
            keep[0][row(t), :] = shorted[1]
            keep[1][row(t), :] = shorted[2]
        return carry

    lax.fori_loop(0, tokens + margin, step, 0, unroll=2)


def main_kernel(
    tokens, margin, modes, part, q, k, v, c, before, after, taps, rate, weight, state,
    dq, dk, dv, sums, tap_sums,
    w0, w1, w2, w3, gated, grad_mixed, keys, values, mixed, grad_gated, trail, o0, o1, o2,
):
    wide = (w0, w1, w2, w3)
    load_inputs(tokens, margin, (q, k, v, c), before, after, wide)
    short_products(tokens, margin, taps, wide, gated, grad_mixed, (keys, values))
    zero = jnp.zeros((GROUPS, LANES), F32)
    for first in range(0, modes, part):
        some = range(first, first + part)
        decay = [jnp.exp(-rate[n]) for n in some]
        amount = [weight[n] for n in some]

        def total_of(terms):
            terms = list(terms)
            while len(terms) > 1:
                terms = [a + b for a, b in zip(terms[::2], terms[1::2])]
            return terms[0]

        def forward(t, carry):
            x, dots = carry
            u = gated[row(t), :]
            g = grad_mixed[row(t), :]
            x = tuple(decay[n] * x[n] + u for n in range(part))
            for n in range(part):
                trail[row(t * part + n), :] = x[n]
            y = total_of(amount[n] * x[n] for n in range(part))
            if first > 0:
                y = y + mixed[row(t), :]
            mixed[row(t), :] = y
            return (x, tuple(dots[n] + g * x[n] for n in range(part)))

        start = tuple(state[0, n, 0] for n in some)
        x, dots = lax.fori_loop(0, tokens, forward, (start, (zero,) * part), unroll=2)
        for n in range(part):
            sums[0, first + n] = dots[n]
        for t in range(tokens, tokens + margin):
            u = gated[row(t), :]
            x = tuple(decay[n] * x[n] + u for n in range(part))
            y = total_of(amount[n] * x[n] for n in range(part))
            if first > 0:
                y = y + mixed[row(t), :]
            mixed[row(t), :] = y

        def backward(i, carry):
            t = tokens - 1 - i
            h, dots = carry
            g = grad_mixed[row(t), :]
            dots = tuple(dots[n] + trail[row(t * part + n), :] * h[n] for n in range(part))
            h = tuple(decay[n] * h[n] + g for n in range(part))
            y = total_of(amount[n] * h[n] for n in range(part))
            if first > 0:
                y = y + grad_gated[row(t), :]
            grad_gated[row(t), :] = y
            return (h, dots)

        start = tuple(state[0, n, 1] for n in some)
        h, dots = lax.fori_loop(0, tokens, backward, (start, (zero,) * part), unroll=2)
        for n in range(part):
            sums[1, first + n] = decay[n] * dots[n]
        grow = [jnp.exp(rate[n]) for n in some]
        h = start
        for t in range(tokens, tokens + margin):
            y = total_of(amount[n] * h[n] for n in range(part))
            if first > 0:
                y = y + grad_gated[row(t), :]
            grad_gated[row(t), :] = y
            g = grad_mixed[row(t), :]
            h = tuple((h[n] - g) * grow[n] for n in range(part))

    filters = [[taps[i, j] for j in range(margin + 1)] for i in range(3)]
    outs = (o0, o1, o2)

    def grads_at(t):
        m = rounded(mixed[row(t), :])
        gg = rounded(grad_gated[row(t), :])
        return (wide[3][row(t + margin), :] * m, gg * values[row(t), :], gg * keys[row(t), :])

    def finish(i, carry):
        t = tokens - 1 - i
        later, dots = carry
        now = grads_at(t)
        window = (now,) + later
        new = []
        for a in range(3):
            total = filters[a][0] * now[a]
            for j in range(1, margin + 1):
                total = total + filters[a][j] * window[j][a]
            outs[a][row(t), :] = total
            for j in range(margin + 1):
                new.append(dots[a * (margin + 1) + j] + now[a] * wide[a][row(t + margin - j), :])
        return (window[:margin], tuple(new))

    later = tuple(grads_at(tokens + j) for j in range(margin))
    later, dots = lax.fori_loop(0, tokens, finish, (later, (zero,) * (3 * (margin + 1))), unroll=2)
    for a in range(3):
        for j in range(margin + 1):
            tap_sums[a, j] = dots[a * (margin + 1) + j]
    for source, target in zip(outs, (dq, dk, dv)):
        gather_rows(source, target, tokens)


MESH = pl.DeviceIdType.MESH


def partner(d):
    count = lax.axis_size("seq")
    return lax.rem(lax.axis_index("seq") + d, count)


def core_of():
    return lax.rem(lax.axis_index("dp"), 2)


def other_core():
    return lax.axis_index("dp") + 1 - 2 * core_of()


def greet():
    count = lax.axis_size("seq")
    barrier = pltpu.get_barrier_semaphore()

    def step(d, carry):
        pl.semaphore_signal(barrier, inc=1, device_id={"seq": partner(d)}, device_id_type=MESH)
        return carry

    lax.fori_loop(1, count, step, 0)
    pl.semaphore_signal(barrier, inc=1, device_id={"dp": other_core()}, device_id_type=MESH)
    pl.semaphore_wait(barrier, count)


def remote(source, target, sems, d, device):
    return pltpu.make_async_remote_copy(
        src_ref=source,
        dst_ref=target,
        send_sem=sems.at[0, d],
        recv_sem=sems.at[1, d],
        device_id=device,
        device_id_type=MESH,
    )


class ToAll:

    def __init__(self, source_of, target, sems):
        self.source_of, self.target, self.sems = source_of, target, sems

    def copy(self, d):
        p = partner(d)
        slot = self.target.at[lax.axis_index("seq")]
        return remote(self.source_of(p), slot, self.sems, d, {"seq": p})

    def start(self):
        def step(d, carry):
            self.copy(d).start()
            return carry

        lax.fori_loop(1, lax.axis_size("seq"), step, 0)

    def wait(self):
        def step(d, carry):
            self.copy(d).wait()
            return carry

        lax.fori_loop(1, lax.axis_size("seq"), step, 0)


def to_other_core(ref, sems, d):
    return remote(ref, ref, sems, d, {"dp": other_core()})


def front_kernel(
    tokens, margin, modes, blocks, own,
    q, k, v, c, mine, before, after, taps,
    modal, got_before, got_after, carried,
    w0, w1, w2, w3, gated, grad_mixed, slots, table, left, right, state, got, sent, landed,
    slot_sems, halo_sems, swap_sems, out_sems, back_sems,
):
    me = lax.axis_index("seq")
    count = lax.axis_size("seq")
    core = core_of()
    units = 2 * modes // count
    wide = (w0, w1, w2, w3)
    greet()
    halos = [
        remote(before, left, halo_sems, 0, {"seq": partner(1)}),
        remote(after, right, halo_sems, 1, {"seq": partner(count - 1)}),
    ]
    for copy in halos:
        copy.start()
    gathering = ToAll(lambda p: mine.at[core], slots.at[core], slot_sems)
    gathering.start()
    slots[core, me] = mine[core]
    for b in range(blocks):
        for i, x in enumerate((q, k, v, c)):
            spread_rows(x, wide[i].at[b], margin, tokens, b * WIDE)
    gathering.wait()
    copy = to_other_core(slots.at[core], swap_sems, 0)
    copy.start()
    for halo in halos:
        halo.wait()
    got_before[...] = jnp.where(me > 0, left[...].astype(F32), 0.0).astype(BF16)
    got_after[...] = jnp.where(me < count - 1, right[...].astype(F32), 0.0).astype(BF16)
    copy.wait()

    def arrange(n, carry):
        for i in range(2):
            for p in range(count):
                table[i, n, p * own : (p + 1) * own, :] = slots[i, p, n]
        return carry

    lax.fori_loop(0, modes, arrange, 0)
    modal[...] = table[...]
    zero = jnp.zeros((GROUPS, LANES), F32)

    def out_copies(b):
        return ToAll(lambda p: state.at[b, p], got.at[b], out_sems.at[b])

    def back_copies(b):
        return ToAll(lambda p: sent.at[b, p], landed.at[b], back_sems.at[b])

    def combine(b):
        out_copies(b).wait()
        cols = slice(b * GROUPS, (b + 1) * GROUPS)
        for unit in range(units):
            which = me * units + unit
            backward = lax.rem(which, 2)
            factor = jnp.exp(-tokens * table[0, lax.div(which, 2), cols, :])

            def step(p, total):
                place = p + backward * (count - 1 - 2 * p)
                sent[b, place, unit] = total
                return factor * total + got[b, place, unit]

            lax.fori_loop(0, count, step, zero, unroll=4)
        back_copies(b).start()
        landed[b, me] = sent[b, me]

    for b in range(blocks):
        cols = slice(b * GROUPS, (b + 1) * GROUPS)
        mine_wide = [x.at[b] for x in wide]
        for i in range(4):
            for j in range(margin):
                if i < 3:
                    mine_wide[i][row(j), :] = got_before[i, j, cols, :].astype(F32)
                mine_wide[i][row(margin + tokens + j), :] = got_after[i, j, cols, :].astype(F32)
        short_products(tokens, margin, taps[:, :, cols, :], mine_wide, gated, grad_mixed, None)
        decay = [jnp.exp(-table[0, n, cols, :]) for n in range(modes)]

        def step(t, carry):
            ahead, back = carry
            u = gated[row(t), :]
            g = grad_mixed[row(tokens - 1 - t), :]
            return (
                tuple(decay[n] * ahead[n] + u for n in range(modes)),
                tuple(decay[n] * back[n] + g for n in range(modes)),
            )

        ends = lax.fori_loop(0, tokens, step, ((zero,) * modes, (zero,) * modes), unroll=2)
        for n in range(modes):
            for i in range(2):
                unit = 2 * n + i
                state[b, unit // units, unit % units] = ends[i][n]
        out_copies(b).start()
        got[b, me] = state[b, me]
        if b > 0:
            combine(b - 1)
    combine(blocks - 1)
    for b in range(blocks):
        back_copies(b).wait()
    carried[...] = landed[...]


def reduce_part(packed, other, summed, got, sems, swap_sems):
    me = lax.axis_index("seq")
    core = core_of()
    copy = remote(packed.at[1 - core], other, swap_sems, 0, {"dp": other_core()})
    copy.start()
    copy.wait()
    summed[...] = packed[core] + other[...]
    copies = ToAll(lambda p: summed.at[p], got, sems)
    copies.start()
    got[me] = summed[me]
    copies.wait()
    total = got[0]
    for p in range(1, got.shape[0]):
        total = total + got[p]
    return total


def share_part(total, sums, taps, both, slots, sems, swap_sems):
    me = lax.axis_index("seq")
    core = core_of()
    count, tap_rows = slots.shape[1:3]
    sum_rows = total.shape[0] - tap_rows
    both[core] = total[:sum_rows]
    slots[core, me] = total[sum_rows:]
    copies = ToAll(lambda p: slots.at[core, me], slots.at[core], sems)
    copies.start()
    first = to_other_core(both.at[core], swap_sems, 1)
    first.start()
    copies.wait()
    second = to_other_core(slots.at[core], swap_sems, 2)
    second.start()
    first.wait()
    second.wait()
    sums[...] = both[...]
    taps[...] = slots[...]


def reduce_kernel(packed, out, other, summed, got, sems, swap_sems):
    greet()
    out[...] = reduce_part(packed, other, summed, got, sems, swap_sems)


def share_kernel(half, sums, taps, both, slots, sems, swap_sems):
    greet()
    share_part(half[...], sums, taps, both, slots, sems, swap_sems)


def end_kernel(packed, sums, taps, other, summed, got, both, slots, sems, share_sems, swap_sems):
    greet()
    total = reduce_part(packed, other, summed, got, sems, swap_sems)
    share_part(total, sums, taps, both, slots, share_sems, swap_sems)


def comm_call(kernel, ident, name, shapes, scratch):
    return pl.pallas_call(
        kernel,
        out_shape=shapes,
        scratch_shapes=scratch,
        compiler_params=pltpu.CompilerParams(
            collective_id=ident, has_side_effects=True, vmem_limit_bytes=56 << 20
        ),
        name=name,
    )


def body(query_rows, key_rows, value_rows, cotangent, short_filter, residue, decay_rate):
    batch, tokens, width = query_rows.shape
    assert batch == 1
    margin = short_filter.shape[1] - 1
    modes = residue.shape[1]
    count = lax.axis_size("seq")
    own = residue.shape[0] // LANES
    tiles = width // LANES
    blocks = width // WIDE
    assert 2 * modes % count == 0
    units = 2 * modes // count
    length = tokens * count
    vmem = 56 << 20

    root = jnp.sqrt(-jnp.expm1(-2.0 * decay_rate))
    each = pltpu.SemaphoreType.DMA((2, count))
    each_block = pltpu.SemaphoreType.DMA((blocks, 2, count))
    few = pltpu.SemaphoreType.DMA((2, 3))
    mine = jnp.stack([decay_rate.T, (residue * root).T]).reshape(2, modes, own, LANES)
    rows = (query_rows, key_rows, value_rows, cotangent)
    before = jnp.stack([x[0, tokens - margin :] for x in rows[:3]])
    before = before.reshape(3, margin, tiles, LANES)
    after = jnp.stack([x[0, :margin] for x in rows]).reshape(4, margin, tiles, LANES)
    taps = short_filter.reshape(3, margin + 1, tiles, LANES)

    def scratch(n, *lead):
        return pltpu.VMEM(lead + (n * GROUPS, LANES), F32)

    def vmem_like(shape):
        return pltpu.VMEM(shape, F32)

    moving = (blocks, count, units, GROUPS, LANES)
    modal, before, after, state = comm_call(
        functools.partial(front_kernel, tokens, margin, modes, blocks, own),
        0,
        "block_states",
        [
            jax.ShapeDtypeStruct((2, modes, tiles, LANES), F32),
            jax.ShapeDtypeStruct(before.shape, BF16),
            jax.ShapeDtypeStruct(after.shape, BF16),
            jax.ShapeDtypeStruct(moving, F32),
        ],
        [scratch(tokens + 2 * margin, blocks)] * 4
        + [scratch(tokens + margin)] * 2
        + [
            vmem_like((2, count, modes, own, LANES)),
            vmem_like((2, modes, tiles, LANES)),
            pltpu.VMEM(before.shape, BF16),
            pltpu.VMEM(after.shape, BF16),
        ]
        + [vmem_like(moving)] * 4
        + [each, few, few, each_block, each_block],
    )(*rows, mine, before, after, taps)
    rate, weight = modal
    state = state.reshape(blocks, modes, 2, GROUPS, LANES)

    rows_spec = pl.BlockSpec((1, tokens, WIDE), lambda i: (0, 0, i))

    def tile_spec(*lead):
        zeros = (0,) * len(lead)
        return pl.BlockSpec(lead + (GROUPS, LANES), lambda i: zeros + (i, 0))

    state_spec = pl.BlockSpec((1, modes, 2, GROUPS, LANES), lambda i: (i, 0, 0, 0, 0))
    params = pltpu.CompilerParams(vmem_limit_bytes=vmem)
    head = [rows_spec] * 4 + [tile_spec(3, margin), tile_spec(4, margin), tile_spec(3, margin + 1), tile_spec(modes)]
    wide = [scratch(tokens + 2 * margin)] * 4
    shapes = [jax.ShapeDtypeStruct(query_rows.shape, BF16)] * 3
    dq, dk, dv, sums, tap_sums = pl.pallas_call(
        functools.partial(main_kernel, tokens, margin, modes, modes // 2),
        grid=(blocks,),
        in_specs=head + [tile_spec(modes), state_spec],
        out_specs=[rows_spec] * 3 + [tile_spec(2, modes), tile_spec(3, margin + 1)],
        out_shape=shapes
        + [
            jax.ShapeDtypeStruct((2, modes, tiles, LANES), F32),
            jax.ShapeDtypeStruct((3, margin + 1, tiles, LANES), F32),
        ],
        scratch_shapes=wide
        + [scratch(tokens + margin)] * 6
        + [scratch(tokens * modes // 2)]
        + [scratch(tokens)] * 3,
        compiler_params=params,
        name="mixer",
    )(*rows, before, after, taps, rate, weight, state)

    tap_terms = 3 * (margin + 1) * own
    tap_rows = -(-tap_terms // 16) * 8
    sums = sums.reshape(2, modes, count, own, LANES).transpose(0, 2, 1, 3, 4)
    sums = sums.reshape(2, count, modes * own, LANES)
    tap_sums = tap_sums.reshape(-1, count, own, LANES).transpose(1, 0, 2, 3)
    tap_sums = tap_sums.reshape(count, tap_terms, LANES)
    tap_sums = jnp.pad(tap_sums, ((0, 0), (0, 2 * tap_rows - tap_terms), (0, 0)))
    tap_sums = tap_sums.reshape(count, 2, tap_rows, LANES).transpose(1, 0, 2, 3)
    packed = jnp.concatenate([sums, tap_sums], axis=2)
    half = packed.shape[2]
    blocked = [vmem_like((count, half, LANES))] * 3
    whole = [(2, modes * own, LANES), (2, count, tap_rows, LANES)]
    results = [jax.ShapeDtypeStruct(shape, F32) for shape in whole]
    landing = [vmem_like(shape) for shape in whole]
    cores = lax.axis_size("dp")
    if cores == 2:
        reduced, filter_grad = comm_call(
            end_kernel, 1, "sum_gradients", results, blocked + landing + [each, each, few]
        )(packed)
    else:
        reduced = comm_call(
            reduce_kernel,
            1,
            "reduce_sums",
            jax.ShapeDtypeStruct((half, LANES), F32),
            blocked + [each, few],
        )(packed)
        groups = [[j for j in range(cores) if j % 2 == i] for i in range(2)]
        reduced = lax.psum(reduced, "dp", axis_index_groups=groups)
        reduced, filter_grad = comm_call(
            share_kernel, 2, "share_sums", results, landing + [each, few]
        )(reduced)
    factor = 1.0 / math.sqrt(batch * cores * length)
    reduced = reduced * factor
    filter_grad = filter_grad.transpose(1, 0, 2, 3).reshape(count, 2 * tap_rows, LANES)
    filter_grad = filter_grad[:, :tap_terms] * factor
    filter_grad = filter_grad.reshape(count, 3, margin + 1, own * LANES).transpose(1, 2, 0, 3)
    filter_grad = filter_grad.reshape(3, margin + 1, width)
    first_sum, second_sum = (
        reduced.reshape(2, modes, own * LANES).transpose(0, 2, 1)
    )
    residue_grad = root * first_sum
    rate_grad = (
        residue * jnp.exp(-2.0 * decay_rate) / root * first_sum - residue * root * second_sum
    )
    return (dq, dk, dv, filter_grad, residue_grad, decay_rate * rate_grad)


def solution(mesh):
    rows = P("dp", "seq", None)
    modes = P("seq", None)
    return jax.shard_map(
        body,
        mesh=mesh,
        in_specs=(rows, rows, rows, rows, P(), modes, modes),
        out_specs=(rows, rows, rows, P(), modes, modes),
        check_vma=False,
    )
```

```python
import functools
import math

import jax
import jax.numpy as jnp
from jax import lax
from jax.experimental import pallas as pl
from jax.experimental.pallas import tpu as pltpu
from jax.sharding import PartitionSpec as P

LANES = 128
GROUPS = 8
WIDE = LANES * GROUPS
F32 = jnp.float32
BF16 = jnp.bfloat16


def row(t):
    start = t * GROUPS
    if not isinstance(t, int):
        start = pl.multiple_of(start, GROUPS)
    return pl.ds(start, GROUPS)


def rounded(values):
    return values.astype(BF16).astype(F32)


def spread_rows(source, target, shift, tokens, base=0):
    def step(i, carry):
        start = pl.multiple_of(i * 16, 16)
        for s in range(GROUPS):
            piece = source[0, pl.ds(start, 16), pl.ds(base + s * LANES, LANES)].astype(F32)
            target[pl.ds((start + shift) * GROUPS + s, 16, stride=GROUPS), :] = piece
        return carry

    lax.fori_loop(0, tokens // 16, step, 0)


def gather_rows(source, target, tokens, base):
    def step(i, carry):
        start = pl.multiple_of(i * 16, 16)
        for s in range(GROUPS):
            piece = source[pl.ds(start * GROUPS + s, 16, stride=GROUPS), :]
            target[0, pl.ds(start, 16), pl.ds(base + s * LANES, LANES)] = piece.astype(BF16)
        return carry

    lax.fori_loop(0, tokens // 16, step, 0)


def short_products(tokens, margin, taps, wide, gated, grad_mixed, keep):
    weights = [[taps[i, j] for j in range(margin + 1)] for i in range(3)]

    def step(t, carry):
        shorted = []
        for i in range(3):
            total = weights[i][0] * wide[i][row(t + margin), :]
            for j in range(1, margin + 1):
                total = total + weights[i][j] * wide[i][row(t + margin - j), :]
            shorted.append(total)
        gated[row(t), :] = rounded(shorted[1] * shorted[2])
        grad_mixed[row(t), :] = rounded(wide[3][row(t + margin), :] * shorted[0])
        if keep is not None:
            keep[0][row(t), :] = shorted[1]
            keep[1][row(t), :] = shorted[2]
        return carry

    lax.fori_loop(0, tokens + margin, step, 0, unroll=2)


def main_block(
    tokens, margin, modes, part, cols, base, taps, rate, weight, carry_of,
    dq, dk, dv, sums, tap_sums,
    wide, gated, grad_mixed, keys, values, mixed, grad_gated, trail, outs,
):
    zero = jnp.zeros((GROUPS, LANES), F32)
    for first in range(0, modes, part):
        some = range(first, first + part)
        decay = [jnp.exp(-rate[n, cols, :]) for n in some]
        amount = [weight[n, cols, :] for n in some]

        def total_of(terms):
            terms = list(terms)
            while len(terms) > 1:
                terms = [a + b for a, b in zip(terms[::2], terms[1::2])]
            return terms[0]

        def forward(t, carry):
            x, dots = carry
            u = gated[row(t), :]
            g = grad_mixed[row(t), :]
            x = tuple(decay[n] * x[n] + u for n in range(part))
            for n in range(part):
                trail[row(t * part + n), :] = x[n]
            y = total_of(amount[n] * x[n] for n in range(part))
            if first > 0:
                y = y + mixed[row(t), :]
            mixed[row(t), :] = y
            return (x, tuple(dots[n] + g * x[n] for n in range(part)))

        start = tuple(carry_of(n, 0) for n in some)
        x, dots = lax.fori_loop(0, tokens, forward, (start, (zero,) * part), unroll=2)
        for n in range(part):
            sums[0, first + n, cols, :] = dots[n]
        for t in range(tokens, tokens + margin):
            u = gated[row(t), :]
            x = tuple(decay[n] * x[n] + u for n in range(part))
            y = total_of(amount[n] * x[n] for n in range(part))
            if first > 0:
                y = y + mixed[row(t), :]
            mixed[row(t), :] = y

        def backward(i, carry):
            t = tokens - 1 - i
            h, dots = carry
            g = grad_mixed[row(t), :]
            dots = tuple(dots[n] + trail[row(t * part + n), :] * h[n] for n in range(part))
            h = tuple(decay[n] * h[n] + g for n in range(part))
            y = total_of(amount[n] * h[n] for n in range(part))
            if first > 0:
                y = y + grad_gated[row(t), :]
            grad_gated[row(t), :] = y
            return (h, dots)

        start = tuple(carry_of(n, 1) for n in some)
        h, dots = lax.fori_loop(0, tokens, backward, (start, (zero,) * part), unroll=2)
        for n in range(part):
            sums[1, first + n, cols, :] = decay[n] * dots[n]
        grow = [jnp.exp(rate[n, cols, :]) for n in some]
        h = start
        for t in range(tokens, tokens + margin):
            y = total_of(amount[n] * h[n] for n in range(part))
            if first > 0:
                y = y + grad_gated[row(t), :]
            grad_gated[row(t), :] = y
            g = grad_mixed[row(t), :]
            h = tuple((h[n] - g) * grow[n] for n in range(part))

    filters = [[taps[i, j, cols, :] for j in range(margin + 1)] for i in range(3)]

    def grads_at(t):
        m = rounded(mixed[row(t), :])
        gg = rounded(grad_gated[row(t), :])
        return (wide[3][row(t + margin), :] * m, gg * values[row(t), :], gg * keys[row(t), :])

    def finish(i, carry):
        t = tokens - 1 - i
        later, dots = carry
        now = grads_at(t)
        window = (now,) + later
        new = []
        for a in range(3):
            total = filters[a][0] * now[a]
            for j in range(1, margin + 1):
                total = total + filters[a][j] * window[j][a]
            outs[a][row(t), :] = total
            for j in range(margin + 1):
                new.append(dots[a * (margin + 1) + j] + now[a] * wide[a][row(t + margin - j), :])
        return (window[:margin], tuple(new))

    later = tuple(grads_at(tokens + j) for j in range(margin))
    later, dots = lax.fori_loop(0, tokens, finish, (later, (zero,) * (3 * (margin + 1))), unroll=2)
    for a in range(3):
        for j in range(margin + 1):
            tap_sums[a, j, cols, :] = dots[a * (margin + 1) + j]
    for source, target in zip(outs, (dq, dk, dv)):
        gather_rows(source, target, tokens, base)


MESH = pl.DeviceIdType.MESH


def partner(d):
    count = lax.axis_size("seq")
    return lax.rem(lax.axis_index("seq") + d, count)


def core_of():
    return lax.rem(lax.axis_index("dp"), 2)


def other_core():
    return lax.axis_index("dp") + 1 - 2 * core_of()


def greet():
    count = lax.axis_size("seq")
    barrier = pltpu.get_barrier_semaphore()

    def step(d, carry):
        pl.semaphore_signal(barrier, inc=1, device_id={"seq": partner(d)}, device_id_type=MESH)
        return carry

    lax.fori_loop(1, count, step, 0)
    pl.semaphore_signal(barrier, inc=1, device_id={"dp": other_core()}, device_id_type=MESH)
    pl.semaphore_wait(barrier, count)


def remote(source, target, sems, d, device):
    return pltpu.make_async_remote_copy(
        src_ref=source,
        dst_ref=target,
        send_sem=sems.at[0, d],
        recv_sem=sems.at[1, d],
        device_id=device,
        device_id_type=MESH,
    )


class ToAll:

    def __init__(self, source_of, target, sems):
        self.source_of, self.target, self.sems = source_of, target, sems

    def copy(self, d):
        p = partner(d)
        slot = self.target.at[lax.axis_index("seq")]
        return remote(self.source_of(p), slot, self.sems, d, {"seq": p})

    def start(self):
        def step(d, carry):
            self.copy(d).start()
            return carry

        lax.fori_loop(1, lax.axis_size("seq"), step, 0)

    def wait(self):
        def step(d, carry):
            self.copy(d).wait()
            return carry

        lax.fori_loop(1, lax.axis_size("seq"), step, 0)


def to_other_core(ref, sems, d):
    return remote(ref, ref, sems, d, {"dp": other_core()})


class Level:

    def __init__(self, size, mine, device_of, source_of, target, sems):
        self.size, self.mine, self.device_of = size, mine, device_of
        self.source_of, self.target, self.sems = source_of, target, sems

    def copies(self):
        for d in range(1, self.size):
            j = lax.rem(self.mine + d, self.size)
            device = {"seq": self.device_of(j)}
            yield remote(self.source_of(j), self.target.at[self.mine], self.sems, d, device)

    def start(self):
        for copy in self.copies():
            copy.start()

    def wait(self):
        for copy in self.copies():
            copy.wait()


def mixer_kernel(
    tokens, margin, modes, blocks, own, inner,
    q, k, v, c, mine, taps,
    dq, dk, dv, sums, tap_sums,
    w0, w1, w2, w3, gated, grad_mixed, keys, values, mixed, grad_gated, trail, o0, o1, o2,
    slots, table, before, after, left, right, state, got, total, planes, sent, landed,
    slot_sems, halo_sems, swap_sems, out_sems, plane_sems, back_sems,
):
    me = lax.axis_index("seq")
    count = lax.axis_size("seq")
    core = core_of()
    outer = count // inner
    per = modes // inner
    low = lax.rem(me, inner)
    high = lax.div(me, inner)
    wide = (w0, w1, w2, w3)
    zero = jnp.zeros((GROUPS, LANES), F32)
    greet()
    gathering = ToAll(lambda p: mine.at[core], slots.at[core], slot_sems)
    gathering.start()
    slots[core, me] = mine[core]
    for b in range(blocks):
        cols = slice(b * GROUPS, (b + 1) * GROUPS)
        for i, x in enumerate((q, k, v, c)):
            spread_rows(x, wide[i].at[b], margin, tokens, b * WIDE)
            for j in range(margin):
                if i < 3:
                    before[i, j, cols, :] = wide[i][b, row(tokens + j), :]
                after[i, j, cols, :] = wide[i][b, row(margin + j), :]
    halos = [
        remote(before, left, halo_sems, 0, {"seq": partner(1)}),
        remote(after, right, halo_sems, 1, {"seq": partner(count - 1)}),
    ]
    for copy in halos:
        copy.start()
    gathering.wait()
    copy = to_other_core(slots.at[core], swap_sems, 0)
    copy.start()
    for halo in halos:
        halo.wait()
    for b in range(blocks):
        cols = slice(b * GROUPS, (b + 1) * GROUPS)
        for i in range(4):
            for j in range(margin):
                if i < 3:
                    wide[i][b, row(j), :] = jnp.where(me > 0, left[i, j, cols, :], 0.0)
                wide[i][b, row(margin + tokens + j), :] = jnp.where(
                    me < count - 1, right[i, j, cols, :], 0.0
                )
    copy.wait()

    def arrange(n, carry):
        for i in range(2):
            for p in range(count):
                table[i, n, p * own : (p + 1) * own, :] = slots[i, p, n]
        return carry

    lax.fori_loop(0, modes, arrange, 0)
    rate, weight = table.at[0], table.at[1]

    def near(source, target, sems, b):
        return Level(
            inner, low, lambda j: high * inner + j, lambda j: source.at[b, j], target.at[b], sems.at[b]
        )

    def far(b):
        def source_of(j):
            return total.at[b, jnp.where(j > high, 0, 1)]

        return Level(
            outer, high, lambda j: j * inner + low, source_of, planes.at[b], plane_sems.at[b]
        )

    def power(n, cols, times):
        return jnp.exp(-times * tokens * table[0, low * per + n, cols, :])

    def add_group(b):
        near(state, got, out_sems, b).wait()
        cols = slice(b * GROUPS, (b + 1) * GROUPS)
        for n in range(per):
            factor = power(n, cols, 1)
            ahead = got[b, 0, 0, n]
            back = got[b, inner - 1, 1, n]
            for j in range(1, inner):
                ahead = factor * ahead + got[b, j, 0, n]
                back = factor * back + got[b, inner - 1 - j, 1, n]
            total[b, 0, n] = ahead
            total[b, 1, n] = back
        far(b).start()

    def give_back(b):
        far(b).wait()
        cols = slice(b * GROUPS, (b + 1) * GROUPS)
        for n in range(per):
            factor = power(n, cols, 1)
            jump = power(n, cols, inner)
            ahead = lax.fori_loop(0, high, lambda z, x: jump * x + planes[b, z, n], zero)
            back = lax.fori_loop(
                high + 1, outer, lambda z, x: jump * x + planes[b, outer + high - z, n], zero
            )
            for j in range(inner):
                sent[b, j, 0, n] = ahead
                ahead = factor * ahead + got[b, j, 0, n]
                sent[b, inner - 1 - j, 1, n] = back
                back = factor * back + got[b, inner - 1 - j, 1, n]
        near(sent, landed, back_sems, b).start()
        landed[b, low] = sent[b, low]

    for b in range(blocks):
        cols = slice(b * GROUPS, (b + 1) * GROUPS)
        u_ref, g_ref = gated.at[b], grad_mixed.at[b]
        short_products(
            tokens, margin, taps[:, :, cols, :], [x.at[b] for x in wide], u_ref, g_ref,
            (keys.at[b], values.at[b]),
        )
        decay = [jnp.exp(-rate[n, cols, :]) for n in range(modes)]

        def step(t, carry):
            ahead, back = carry
            u = u_ref[row(t), :]
            g = g_ref[row(tokens - 1 - t), :]
            return (
                tuple(decay[n] * ahead[n] + u for n in range(modes)),
                tuple(decay[n] * back[n] + g for n in range(modes)),
            )

        ends = lax.fori_loop(0, tokens, step, ((zero,) * modes, (zero,) * modes), unroll=2)
        for n in range(modes):
            for i in range(2):
                state[b, n // per, i, n % per] = ends[i][n]
        near(state, got, out_sems, b).start()
        got[b, low] = state[b, low]
        if b > 0:
            add_group(b - 1)
        if b > 1:
            give_back(b - 2)
    add_group(blocks - 1)
    if blocks > 1:
        give_back(blocks - 2)
    for b in range(blocks):
        if blocks == 1:
            give_back(b)
        near(sent, landed, back_sems, b).wait()
        main_block(
            tokens, margin, modes, modes // 2, slice(b * GROUPS, (b + 1) * GROUPS), b * WIDE,
            taps, rate, weight, lambda n, i: landed[b, n // per, i, n % per],
            dq, dk, dv, sums, tap_sums,
            [x.at[b] for x in wide], gated.at[b], grad_mixed.at[b], keys.at[b], values.at[b],
            mixed, grad_gated, trail, (o0, o1, o2),
        )
        if b == 0 and blocks > 1:
            give_back(blocks - 1)


def reduce_part(packed, other, summed, got, sems, swap_sems):
    me = lax.axis_index("seq")
    core = core_of()
    copy = remote(packed.at[1 - core], other, swap_sems, 0, {"dp": other_core()})
    copy.start()
    copy.wait()
    summed[...] = packed[core] + other[...]
    copies = ToAll(lambda p: summed.at[p], got, sems)
    copies.start()
    got[me] = summed[me]
    copies.wait()
    total = got[0]
    for p in range(1, got.shape[0]):
        total = total + got[p]
    return total


def share_part(total, sums, taps, both, slots, sems, swap_sems):
    me = lax.axis_index("seq")
    core = core_of()
    count, tap_rows = slots.shape[1:3]
    sum_rows = total.shape[0] - tap_rows
    both[core] = total[:sum_rows]
    slots[core, me] = total[sum_rows:]
    copies = ToAll(lambda p: slots.at[core, me], slots.at[core], sems)
    copies.start()
    first = to_other_core(both.at[core], swap_sems, 1)
    first.start()
    copies.wait()
    second = to_other_core(slots.at[core], swap_sems, 2)
    second.start()
    first.wait()
    second.wait()
    sums[...] = both[...]
    taps[...] = slots[...]


def reduce_kernel(packed, out, other, summed, got, sems, swap_sems):
    greet()
    out[...] = reduce_part(packed, other, summed, got, sems, swap_sems)


def share_kernel(half, sums, taps, both, slots, sems, swap_sems):
    greet()
    share_part(half[...], sums, taps, both, slots, sems, swap_sems)


def end_kernel(packed, sums, taps, other, summed, got, both, slots, sems, share_sems, swap_sems):
    greet()
    total = reduce_part(packed, other, summed, got, sems, swap_sems)
    share_part(total, sums, taps, both, slots, share_sems, swap_sems)


def comm_call(kernel, ident, name, shapes, scratch):
    return pl.pallas_call(
        kernel,
        out_shape=shapes,
        scratch_shapes=scratch,
        compiler_params=pltpu.CompilerParams(
            collective_id=ident, has_side_effects=True, vmem_limit_bytes=56 << 20
        ),
        name=name,
    )


def body(query_rows, key_rows, value_rows, cotangent, short_filter, residue, decay_rate):
    batch, tokens, width = query_rows.shape
    assert batch == 1
    margin = short_filter.shape[1] - 1
    modes = residue.shape[1]
    count = lax.axis_size("seq")
    own = residue.shape[0] // LANES
    tiles = width // LANES
    blocks = width // WIDE
    inner = 4
    assert count % inner == 0 and modes % inner == 0
    outer, per = count // inner, modes // inner
    length = tokens * count

    root = jnp.sqrt(-jnp.expm1(-2.0 * decay_rate))
    each = pltpu.SemaphoreType.DMA((2, count))
    few = pltpu.SemaphoreType.DMA((2, 3))
    mine = jnp.stack([decay_rate.T, (residue * root).T]).reshape(2, modes, own, LANES)
    rows = (query_rows, key_rows, value_rows, cotangent)
    taps = short_filter.reshape(3, margin + 1, tiles, LANES)

    def scratch(n, *lead):
        return pltpu.VMEM(lead + (n * GROUPS, LANES), F32)

    def vmem_like(shape):
        return pltpu.VMEM(shape, F32)

    group = (blocks, inner, 2, per, GROUPS, LANES)
    levels = pltpu.SemaphoreType.DMA((blocks, 2, inner))
    far_level = pltpu.SemaphoreType.DMA((blocks, 2, outer))
    halo = [vmem_like((i, margin, tiles, LANES)) for i in (3, 4)]
    dq, dk, dv, sums, tap_sums = comm_call(
        functools.partial(mixer_kernel, tokens, margin, modes, blocks, own, inner),
        0,
        "mixer",
        [jax.ShapeDtypeStruct(query_rows.shape, BF16)] * 3
        + [
            jax.ShapeDtypeStruct((2, modes, tiles, LANES), F32),
            jax.ShapeDtypeStruct((3, margin + 1, tiles, LANES), F32),
        ],
        [scratch(tokens + 2 * margin, blocks)] * 4
        + [scratch(tokens + margin, blocks)] * 4
        + [scratch(tokens + margin)] * 2
        + [scratch(tokens * modes // 2)]
        + [scratch(tokens)] * 3
        + [vmem_like((2, count, modes, own, LANES)), vmem_like((2, modes, tiles, LANES))]
        + halo * 2
        + [vmem_like(group)] * 2
        + [
            vmem_like((blocks, 2, per, GROUPS, LANES)),
            vmem_like((blocks, outer, per, GROUPS, LANES)),
        ]
        + [vmem_like(group)] * 2
        + [each, few, few, levels, far_level, levels],
    )(*rows, mine, taps)

    tap_terms = 3 * (margin + 1) * own
    tap_rows = -(-tap_terms // 16) * 8
    sums = sums.reshape(2, modes, count, own, LANES).transpose(0, 2, 1, 3, 4)
    sums = sums.reshape(2, count, modes * own, LANES)
    tap_sums = tap_sums.reshape(-1, count, own, LANES).transpose(1, 0, 2, 3)
    tap_sums = tap_sums.reshape(count, tap_terms, LANES)
    tap_sums = jnp.pad(tap_sums, ((0, 0), (0, 2 * tap_rows - tap_terms), (0, 0)))
    tap_sums = tap_sums.reshape(count, 2, tap_rows, LANES).transpose(1, 0, 2, 3)
    packed = jnp.concatenate([sums, tap_sums], axis=2)
    half = packed.shape[2]
    blocked = [vmem_like((count, half, LANES))] * 3
    whole = [(2, modes * own, LANES), (2, count, tap_rows, LANES)]
    results = [jax.ShapeDtypeStruct(shape, F32) for shape in whole]
    landing = [vmem_like(shape) for shape in whole]
    cores = lax.axis_size("dp")
    if cores == 2:
        reduced, filter_grad = comm_call(
            end_kernel, 1, "sum_gradients", results, blocked + landing + [each, each, few]
        )(packed)
    else:
        reduced = comm_call(
            reduce_kernel,
            1,
            "reduce_sums",
            jax.ShapeDtypeStruct((half, LANES), F32),
            blocked + [each, few],
        )(packed)
        groups = [[j for j in range(cores) if j % 2 == i] for i in range(2)]
        reduced = lax.psum(reduced, "dp", axis_index_groups=groups)
        reduced, filter_grad = comm_call(
            share_kernel, 2, "share_sums", results, landing + [each, few]
        )(reduced)
    factor = 1.0 / math.sqrt(batch * cores * length)
    reduced = reduced * factor
    filter_grad = filter_grad.transpose(1, 0, 2, 3).reshape(count, 2 * tap_rows, LANES)
    filter_grad = filter_grad[:, :tap_terms] * factor
    filter_grad = filter_grad.reshape(count, 3, margin + 1, own * LANES).transpose(1, 2, 0, 3)
    filter_grad = filter_grad.reshape(3, margin + 1, width)
    first_sum, second_sum = (
        reduced.reshape(2, modes, own * LANES).transpose(0, 2, 1)
    )
    residue_grad = root * first_sum
    rate_grad = (
        residue * jnp.exp(-2.0 * decay_rate) / root * first_sum - residue * root * second_sum
    )
    return (dq, dk, dv, filter_grad, residue_grad, decay_rate * rate_grad)


def solution(mesh):
    rows = P("dp", "seq", None)
    modes = P("seq", None)
    return jax.shard_map(
        body,
        mesh=mesh,
        in_specs=(rows, rows, rows, rows, P(), modes, modes),
        out_specs=(rows, rows, rows, P(), modes, modes),
        check_vma=False,
    )
```

```python
import functools
import math

import jax
import jax.numpy as jnp
from jax import lax
from jax.experimental import pallas as pl
from jax.experimental.pallas import tpu as pltpu
from jax.sharding import PartitionSpec as P

LANES = 128
GROUPS = 8
WIDE = LANES * GROUPS
F32 = jnp.float32
BF16 = jnp.bfloat16


def row(t):
    start = t * GROUPS
    if not isinstance(t, int):
        start = pl.multiple_of(start, GROUPS)
    return pl.ds(start, GROUPS)


def rounded(values):
    return values.astype(BF16).astype(F32)


def spread_rows(source, target, shift, tokens, base=0):
    def step(i, carry):
        start = pl.multiple_of(i * 16, 16)
        for s in range(GROUPS):
            piece = source[0, pl.ds(start, 16), pl.ds(base + s * LANES, LANES)].astype(F32)
            target[pl.ds((start + shift) * GROUPS + s, 16, stride=GROUPS), :] = piece
        return carry

    lax.fori_loop(0, tokens // 16, step, 0)


def gather_rows(source, target, tokens, base):
    def step(i, carry):
        start = pl.multiple_of(i * 16, 16)
        for s in range(GROUPS):
            piece = source[pl.ds(start * GROUPS + s, 16, stride=GROUPS), :]
            target[0, pl.ds(start, 16), pl.ds(base + s * LANES, LANES)] = piece.astype(BF16)
        return carry

    lax.fori_loop(0, tokens // 16, step, 0)


def short_products(tokens, margin, taps, wide, gated, grad_mixed, keep):
    weights = [[taps[i, j] for j in range(margin + 1)] for i in range(3)]

    def step(t, carry):
        shorted = []
        for i in range(3):
            total = weights[i][0] * wide[i][row(t + margin), :]
            for j in range(1, margin + 1):
                total = total + weights[i][j] * wide[i][row(t + margin - j), :]
            shorted.append(total)
        gated[row(t), :] = rounded(shorted[1] * shorted[2])
        grad_mixed[row(t), :] = rounded(wide[3][row(t + margin), :] * shorted[0])
        if keep is not None:
            keep[0][row(t), :] = shorted[1]
            keep[1][row(t), :] = shorted[2]
        return carry

    lax.fori_loop(0, tokens + margin, step, 0, unroll=4)


def main_block(
    tokens, margin, modes, part, cols, base, taps, rate, weight, carry_of,
    dq, dk, dv, put_sum, put_tap,
    wide, gated, grad_mixed, keys, values, mixed, grad_gated, trail, outs,
):
    zero = jnp.zeros((GROUPS, LANES), F32)
    for first in range(0, modes, part):
        some = range(first, first + part)
        decay = [jnp.exp(-rate[n, cols, :]) for n in some]
        amount = [weight[n, cols, :] for n in some]

        def total_of(terms):
            terms = list(terms)
            while len(terms) > 1:
                terms = [a + b for a, b in zip(terms[::2], terms[1::2])]
            return terms[0]

        def forward(t, carry):
            x, dots = carry
            u = gated[row(t), :]
            g = grad_mixed[row(t), :]
            x = tuple(decay[n] * x[n] + u for n in range(part))
            for n in range(part):
                trail[row(t * part + n), :] = x[n]
            y = total_of(amount[n] * x[n] for n in range(part))
            if first > 0:
                y = y + mixed[row(t), :]
            mixed[row(t), :] = y
            return (x, tuple(dots[n] + g * x[n] for n in range(part)))

        start = tuple(carry_of(n, 0) for n in some)
        x, dots = lax.fori_loop(0, tokens, forward, (start, (zero,) * part), unroll=4)
        for n in range(part):
            put_sum(0, first + n, dots[n])
        for t in range(tokens, tokens + margin):
            u = gated[row(t), :]
            x = tuple(decay[n] * x[n] + u for n in range(part))
            y = total_of(amount[n] * x[n] for n in range(part))
            if first > 0:
                y = y + mixed[row(t), :]
            mixed[row(t), :] = y

        def backward(i, carry):
            t = tokens - 1 - i
            h, dots = carry
            g = grad_mixed[row(t), :]
            dots = tuple(dots[n] + trail[row(t * part + n), :] * h[n] for n in range(part))
            h = tuple(decay[n] * h[n] + g for n in range(part))
            y = total_of(amount[n] * h[n] for n in range(part))
            if first > 0:
                y = y + grad_gated[row(t), :]
            grad_gated[row(t), :] = y
            return (h, dots)

        start = tuple(carry_of(n, 1) for n in some)
        h, dots = lax.fori_loop(0, tokens, backward, (start, (zero,) * part), unroll=4)
        for n in range(part):
            put_sum(1, first + n, decay[n] * dots[n])
        grow = [jnp.exp(rate[n, cols, :]) for n in some]
        h = start
        for t in range(tokens, tokens + margin):
            y = total_of(amount[n] * h[n] for n in range(part))
            if first > 0:
                y = y + grad_gated[row(t), :]
            grad_gated[row(t), :] = y
            g = grad_mixed[row(t), :]
            h = tuple((h[n] - g) * grow[n] for n in range(part))

    filters = [[taps[i, j, cols, :] for j in range(margin + 1)] for i in range(3)]

    def grads_at(t):
        m = rounded(mixed[row(t), :])
        gg = rounded(grad_gated[row(t), :])
        return (wide[3][row(t + margin), :] * m, gg * values[row(t), :], gg * keys[row(t), :])

    def finish(i, carry):
        t = tokens - 1 - i
        later, dots = carry
        now = grads_at(t)
        window = (now,) + later
        new = []
        for a in range(3):
            total = filters[a][0] * now[a]
            for j in range(1, margin + 1):
                total = total + filters[a][j] * window[j][a]
            outs[a][row(t), :] = total
            for j in range(margin + 1):
                new.append(dots[a * (margin + 1) + j] + now[a] * wide[a][row(t + margin - j), :])
        return (window[:margin], tuple(new))

    later = tuple(grads_at(tokens + j) for j in range(margin))
    later, dots = lax.fori_loop(0, tokens, finish, (later, (zero,) * (3 * (margin + 1))), unroll=4)
    for a in range(3):
        for j in range(margin + 1):
            put_tap(a * (margin + 1) + j, dots[a * (margin + 1) + j])
    for source, target in zip(outs, (dq, dk, dv)):
        gather_rows(source, target, tokens, base)


MESH = pl.DeviceIdType.MESH


def partner(d):
    count = lax.axis_size("seq")
    return lax.rem(lax.axis_index("seq") + d, count)


def core_of():
    return lax.rem(lax.axis_index("dp"), 2)


def other_core():
    return lax.axis_index("dp") + 1 - 2 * core_of()


def same_core(d):
    return lax.rem(lax.axis_index("dp") + 2 * d, lax.axis_size("dp"))


def greet():
    count = lax.axis_size("seq")
    barrier = pltpu.get_barrier_semaphore()

    def step(d, carry):
        pl.semaphore_signal(barrier, inc=1, device_id={"seq": partner(d)}, device_id_type=MESH)
        return carry

    lax.fori_loop(1, count, step, 0)
    pl.semaphore_signal(barrier, inc=1, device_id={"dp": other_core()}, device_id_type=MESH)
    chips = lax.axis_size("dp") // 2
    for d in range(1, chips):
        pl.semaphore_signal(barrier, inc=1, device_id={"dp": same_core(d)}, device_id_type=MESH)
    pl.semaphore_wait(barrier, count + chips - 1)


def remote(source, target, sems, d, device):
    return pltpu.make_async_remote_copy(
        src_ref=source,
        dst_ref=target,
        send_sem=sems.at[0, d],
        recv_sem=sems.at[1, d],
        device_id=device,
        device_id_type=MESH,
    )


class ToAll:

    def __init__(self, source_of, target, sems):
        self.source_of, self.target, self.sems = source_of, target, sems

    def copy(self, d):
        p = partner(d)
        slot = self.target.at[lax.axis_index("seq")]
        return remote(self.source_of(p), slot, self.sems, d, {"seq": p})

    def start(self):
        def step(d, carry):
            self.copy(d).start()
            return carry

        lax.fori_loop(1, lax.axis_size("seq"), step, 0)

    def wait(self):
        def step(d, carry):
            self.copy(d).wait()
            return carry

        lax.fori_loop(1, lax.axis_size("seq"), step, 0)


def to_other_core(ref, sems, d):
    return remote(ref, ref, sems, d, {"dp": other_core()})


class Level:

    def __init__(self, size, mine, device_of, source_of, target, sems):
        self.size, self.mine, self.device_of = size, mine, device_of
        self.source_of, self.target, self.sems = source_of, target, sems

    def copies(self):
        for d in range(1, self.size):
            j = lax.rem(self.mine + d, self.size)
            device = self.device_of(j)
            yield remote(self.source_of(j), self.target.at[self.mine], self.sems, d, device)

    def start(self):
        for copy in self.copies():
            copy.start()

    def wait(self):
        for copy in self.copies():
            copy.wait()


def mixer_kernel(
    tokens, margin, modes, blocks, own, inner, scale,
    q, k, v, c, mine, taps,
    dq, dk, dv, sums, tap_sums,
    w0, w1, w2, w3, gated, grad_mixed, keys, values, mixed, grad_gated, trail, o0, o1, o2,
    slots, table, before, after, left, right, state, got, total, planes, sent, landed,
    packed, other, summed, near_got, near_sum, far_got, chip_got, both, shared,
    slot_sems, halo_sems, swap_sems, out_sems, plane_sems, back_sems,
    add_sems, near_sems, far_sems, chip_sems, share_sems,
):
    me = lax.axis_index("seq")
    count = lax.axis_size("seq")
    core = core_of()
    outer = count // inner
    per = modes // inner
    low = lax.rem(me, inner)
    high = lax.div(me, inner)
    wide = (w0, w1, w2, w3)
    zero = jnp.zeros((GROUPS, LANES), F32)
    per_block = outer // blocks
    chips = lax.axis_size("dp") // 2
    sum_rows = modes * own
    tap_count = 3 * (margin + 1)
    first_taps = (tap_count + 1) // 2
    greet()
    gathering = ToAll(lambda p: mine.at[core], slots.at[core], slot_sems)
    gathering.start()
    slots[core, me] = mine[core]
    for b in range(blocks):
        cols = slice(b * GROUPS, (b + 1) * GROUPS)
        for i, x in enumerate((q, k, v, c)):
            spread_rows(x, wide[i].at[b], margin, tokens, b * WIDE)
            for j in range(margin):
                if i < 3:
                    before[i, j, cols, :] = wide[i][b, row(tokens + j), :]
                after[i, j, cols, :] = wide[i][b, row(margin + j), :]
    halos = [
        remote(before, left, halo_sems, 0, {"seq": partner(1)}),
        remote(after, right, halo_sems, 1, {"seq": partner(count - 1)}),
    ]
    for copy in halos:
        copy.start()
    gathering.wait()
    copy = to_other_core(slots.at[core], swap_sems, 0)
    copy.start()
    for halo in halos:
        halo.wait()
    for b in range(blocks):
        cols = slice(b * GROUPS, (b + 1) * GROUPS)
        for i in range(4):
            for j in range(margin):
                if i < 3:
                    wide[i][b, row(j), :] = jnp.where(me > 0, left[i, j, cols, :], 0.0)
                wide[i][b, row(margin + tokens + j), :] = jnp.where(
                    me < count - 1, right[i, j, cols, :], 0.0
                )
    copy.wait()

    def arrange(n, carry):
        for i in range(2):
            for p in range(count):
                table[i, n, p * own : (p + 1) * own, :] = slots[i, p, n]
        return carry

    lax.fori_loop(0, modes, arrange, 0)
    rate, weight = table.at[0], table.at[1]

    def near(source, target, sems, b):
        return Level(
            inner, low, lambda j: {"seq": high * inner + j}, lambda j: source.at[b, j], target.at[b], sems.at[b]
        )

    def far(b):
        def source_of(j):
            return total.at[b, jnp.where(j > high, 0, 1)]

        return Level(
            outer, high, lambda j: {"seq": j * inner + low}, source_of, planes.at[b], plane_sems.at[b]
        )

    def power(n, cols, times):
        return jnp.exp(-times * tokens * table[0, low * per + n, cols, :])

    def add_group(b):
        near(state, got, out_sems, b).wait()
        cols = slice(b * GROUPS, (b + 1) * GROUPS)
        for n in range(per):
            factor = power(n, cols, 1)
            ahead = got[b, 0, 0, n]
            back = got[b, inner - 1, 1, n]
            for j in range(1, inner):
                ahead = factor * ahead + got[b, j, 0, n]
                back = factor * back + got[b, inner - 1 - j, 1, n]
            total[b, 0, n] = ahead
            total[b, 1, n] = back
        far(b).start()

    def give_back(b):
        far(b).wait()
        cols = slice(b * GROUPS, (b + 1) * GROUPS)
        for n in range(per):
            factor = power(n, cols, 1)
            jump = power(n, cols, inner)
            ahead = lax.fori_loop(0, high, lambda z, x: jump * x + planes[b, z, n], zero)
            back = lax.fori_loop(
                high + 1, outer, lambda z, x: jump * x + planes[b, outer + high - z, n], zero
            )
            for j in range(inner):
                sent[b, j, 0, n] = ahead
                ahead = factor * ahead + got[b, j, 0, n]
                sent[b, inner - 1 - j, 1, n] = back
                back = factor * back + got[b, inner - 1 - j, 1, n]
        near(sent, landed, back_sems, b).start()
        landed[b, low] = sent[b, low]

    packed[...] = jnp.zeros_like(packed)

    def put_rows(b, part, start, tile):
        for o in range(per_block * inner):
            target = packed.at[part, b * per_block + o // inner, o % inner]
            target[start : start + own, :] = tile[o * own : (o + 1) * own, :]

    def add_cores(b):
        some = pl.ds(b * per_block, per_block)
        return remote(
            packed.at[1 - core, some], other.at[some], add_sems, b, {"dp": other_core()}
        )

    def near_sums(z):
        return Level(
            inner, low, lambda j: {"seq": high * inner + j},
            lambda j: summed.at[z, j], near_got.at[z], near_sems.at[z],
        )

    far_sums = Level(
        outer, high, lambda j: {"seq": j * inner + low}, lambda j: near_sum.at[j], far_got, far_sems
    )

    def pass_near(b):
        add_cores(b).wait()
        for z in range(b * per_block, (b + 1) * per_block):
            summed[z] = packed[core, z] + other[z]
            near_sums(z).start()
            near_got[z, low] = summed[z, low]

    def pass_far(b):
        for z in range(b * per_block, (b + 1) * per_block):
            near_sums(z).wait()
            terms = near_got[z, 0]
            for j in range(1, inner):
                terms = terms + near_got[z, j]
            near_sum[z] = terms

            @pl.when(high == z)
            def _():
                far_got[z] = terms

            @pl.when(high != z)
            def _():
                d = lax.rem(z - high + outer, outer)
                device = {"seq": z * inner + low}
                remote(near_sum.at[z], far_got.at[high], far_sems, d, device).start()

    for b in range(blocks):
        cols = slice(b * GROUPS, (b + 1) * GROUPS)
        u_ref, g_ref = gated.at[b], grad_mixed.at[b]
        short_products(
            tokens, margin, taps[:, :, cols, :], [x.at[b] for x in wide], u_ref, g_ref,
            (keys.at[b], values.at[b]),
        )
        decay = [jnp.exp(-rate[n, cols, :]) for n in range(modes)]

        def step(t, carry):
            ahead, back = carry
            u = u_ref[row(t), :]
            g = g_ref[row(tokens - 1 - t), :]
            return (
                tuple(decay[n] * ahead[n] + u for n in range(modes)),
                tuple(decay[n] * back[n] + g for n in range(modes)),
            )

        ends = lax.fori_loop(0, tokens, step, ((zero,) * modes, (zero,) * modes), unroll=4)
        for n in range(modes):
            for i in range(2):
                state[b, n // per, i, n % per] = ends[i][n]
        near(state, got, out_sems, b).start()
        got[b, low] = state[b, low]
        if b > 0:
            add_group(b - 1)
        if b > 1:
            give_back(b - 2)
    add_group(blocks - 1)
    if blocks > 1:
        give_back(blocks - 2)
    for b in range(blocks):
        if blocks == 1:
            give_back(b)
        near(sent, landed, back_sems, b).wait()

        def put_sum(i, n, tile):
            put_rows(b, i, n * own, tile)

        def put_tap(n, tile):
            part, place = (0, n) if n < first_taps else (1, n - first_taps)
            put_rows(b, part, sum_rows + place * own, tile)

        main_block(
            tokens, margin, modes, modes // 2, slice(b * GROUPS, (b + 1) * GROUPS), b * WIDE,
            taps, rate, weight, lambda n, i: landed[b, n // per, i, n % per],
            dq, dk, dv, put_sum, put_tap,
            [x.at[b] for x in wide], gated.at[b], grad_mixed.at[b], keys.at[b], values.at[b],
            mixed, grad_gated, trail, (o0, o1, o2),
        )
        if b == 0 and blocks > 1:
            give_back(blocks - 1)
        add_cores(b).start()
        if b > 0:
            pass_near(b - 1)
        if b > 1:
            pass_far(b - 2)
    pass_near(blocks - 1)
    if blocks > 1:
        pass_far(blocks - 2)
    pass_far(blocks - 1)
    far_sums.wait()
    total_rows = far_got[0]
    for z in range(1, outer):
        total_rows = total_rows + far_got[z]
    if chips > 1:
        chip = lax.div(lax.axis_index("dp"), 2)
        chip_got[chip] = total_rows
        level = Level(
            chips, chip, lambda j: {"dp": 2 * j + core},
            lambda j: chip_got.at[chip], chip_got, chip_sems,
        )
        level.start()
        level.wait()
        total_rows = chip_got[0]
        for z in range(1, chips):
            total_rows = total_rows + chip_got[z]
    total_rows = total_rows * scale
    shared[core, me] = total_rows[sum_rows:]
    sharing = ToAll(lambda p: shared.at[core, me], shared.at[core], share_sems)
    sharing.start()
    both[core] = total_rows[:sum_rows]
    swap_sums = to_other_core(both.at[core], swap_sems, 1)
    swap_sums.start()
    sharing.wait()
    swap_taps = to_other_core(shared.at[core], swap_sems, 2)
    swap_taps.start()
    swap_sums.wait()
    sums[...] = both[...]
    swap_taps.wait()
    for n in range(tap_count):
        part, place = (0, n) if n < first_taps else (1, n - first_taps)
        for p in range(count):
            tap_sums[n, p * own : (p + 1) * own, :] = shared[
                part, p, place * own : (place + 1) * own, :
            ]


def comm_call(kernel, ident, name, shapes, scratch):
    return pl.pallas_call(
        kernel,
        out_shape=shapes,
        scratch_shapes=scratch,
        compiler_params=pltpu.CompilerParams(
            collective_id=ident, has_side_effects=True, vmem_limit_bytes=56 << 20
        ),
        name=name,
    )


def body(query_rows, key_rows, value_rows, cotangent, short_filter, residue, decay_rate):
    batch, tokens, width = query_rows.shape
    assert batch == 1
    margin = short_filter.shape[1] - 1
    modes = residue.shape[1]
    count = lax.axis_size("seq")
    own = residue.shape[0] // LANES
    tiles = width // LANES
    blocks = width // WIDE
    inner = 4
    assert count % inner == 0 and modes % inner == 0
    outer, per = count // inner, modes // inner
    length = tokens * count

    root = jnp.sqrt(-jnp.expm1(-2.0 * decay_rate))
    each = pltpu.SemaphoreType.DMA((2, count))
    few = pltpu.SemaphoreType.DMA((2, 3))
    cores = lax.axis_size("dp")
    scale = 1.0 / math.sqrt(batch * cores * length)
    tap_count = 3 * (margin + 1)
    tap_rows = -(-((tap_count + 1) // 2 * own) // 8) * 8
    rows_each = modes * own + tap_rows
    mine = jnp.stack([decay_rate.T, (residue * root).T]).reshape(2, modes, own, LANES)
    rows = (query_rows, key_rows, value_rows, cotangent)
    taps = short_filter.reshape(3, margin + 1, tiles, LANES)

    def scratch(n, *lead):
        return pltpu.VMEM(lead + (n * GROUPS, LANES), F32)

    def vmem_like(shape):
        return pltpu.VMEM(shape, F32)

    group = (blocks, inner, 2, per, GROUPS, LANES)
    levels = pltpu.SemaphoreType.DMA((blocks, 2, inner))
    far_level = pltpu.SemaphoreType.DMA((blocks, 2, outer))
    halo = [vmem_like((i, margin, tiles, LANES)) for i in (3, 4)]
    dq, dk, dv, sums, tap_sums = comm_call(
        functools.partial(mixer_kernel, tokens, margin, modes, blocks, own, inner, scale),
        0,
        "mixer",
        [jax.ShapeDtypeStruct(query_rows.shape, BF16)] * 3
        + [
            jax.ShapeDtypeStruct((2, modes * own, LANES), F32),
            jax.ShapeDtypeStruct((tap_count, tiles, LANES), F32),
        ],
        [scratch(tokens + 2 * margin, blocks)] * 4
        + [scratch(tokens + margin, blocks)] * 4
        + [scratch(tokens + margin)] * 2
        + [scratch(tokens * modes // 2)]
        + [scratch(tokens)] * 3
        + [vmem_like((2, count, modes, own, LANES)), vmem_like((2, modes, tiles, LANES))]
        + halo * 2
        + [vmem_like(group)] * 2
        + [
            vmem_like((blocks, 2, per, GROUPS, LANES)),
            vmem_like((blocks, outer, per, GROUPS, LANES)),
        ]
        + [vmem_like(group)] * 2
        + [
            vmem_like((2, outer, inner, rows_each, LANES)),
            vmem_like((outer, inner, rows_each, LANES)),
            vmem_like((outer, inner, rows_each, LANES)),
            vmem_like((outer, inner, rows_each, LANES)),
            vmem_like((outer, rows_each, LANES)),
            vmem_like((outer, rows_each, LANES)),
            vmem_like((max(cores // 2, 1), rows_each, LANES)),
            vmem_like((2, modes * own, LANES)),
            vmem_like((2, count, tap_rows, LANES)),
        ]
        + [each, few, few, levels, far_level, levels]
        + [
            pltpu.SemaphoreType.DMA((2, blocks)),
            pltpu.SemaphoreType.DMA((outer, 2, inner)),
            pltpu.SemaphoreType.DMA((2, outer)),
            pltpu.SemaphoreType.DMA((2, max(cores // 2, 1))),
            each,
        ],
    )(*rows, mine, taps)

    filter_grad = tap_sums.reshape(3, margin + 1, width)
    first_sum, second_sum = (
        sums.reshape(2, modes, own * LANES).transpose(0, 2, 1)
    )
    residue_grad = root * first_sum
    rate_grad = (
        residue * jnp.exp(-2.0 * decay_rate) / root * first_sum - residue * root * second_sum
    )
    return (dq, dk, dv, filter_grad, residue_grad, decay_rate * rate_grad)


def solution(mesh):
    rows = P("dp", "seq", None)
    modes = P("seq", None)
    return jax.shard_map(
        body,
        mesh=mesh,
        in_specs=(rows, rows, rows, rows, P(), modes, modes),
        out_specs=(rows, rows, rows, P(), modes, modes),
        check_vma=False,
    )
```

```python
import functools
import math

import jax
import jax.numpy as jnp
from jax import lax
from jax.experimental import pallas as pl
from jax.experimental.pallas import tpu as pltpu
from jax.sharding import PartitionSpec as P

LANES = 128
GROUPS = 8
WIDE = LANES * GROUPS
F32 = jnp.float32
BF16 = jnp.bfloat16


def row(t):
    start = t * GROUPS
    if not isinstance(t, int):
        start = pl.multiple_of(start, GROUPS)
    return pl.ds(start, GROUPS)


def rounded(values):
    return values.astype(BF16).astype(F32)


def spread_rows(source, target, shift, tokens, base=0):
    def step(i, carry):
        start = pl.multiple_of(i * 16, 16)
        for s in range(GROUPS):
            piece = source[0, pl.ds(start, 16), pl.ds(base + s * LANES, LANES)].astype(F32)
            target[pl.ds((start + shift) * GROUPS + s, 16, stride=GROUPS), :] = piece
        return carry

    lax.fori_loop(0, tokens // 16, step, 0)


def gather_rows(source, target, tokens, base):
    def step(i, carry):
        start = pl.multiple_of(i * 16, 16)
        for s in range(GROUPS):
            piece = source[pl.ds(start * GROUPS + s, 16, stride=GROUPS), :]
            target[0, pl.ds(start, 16), pl.ds(base + s * LANES, LANES)] = piece.astype(BF16)
        return carry

    lax.fori_loop(0, tokens // 16, step, 0)


def short_products(tokens, margin, taps, wide, gated, grad_mixed, keep):
    weights = [[taps[i, j] for j in range(margin + 1)] for i in range(3)]

    def step(t, carry):
        shorted = []
        for i in range(3):
            total = weights[i][0] * wide[i][row(t + margin), :]
            for j in range(1, margin + 1):
                total = total + weights[i][j] * wide[i][row(t + margin - j), :]
            shorted.append(total)
        gated[row(t), :] = rounded(shorted[1] * shorted[2])
        grad_mixed[row(t), :] = rounded(wide[3][row(t + margin), :] * shorted[0])
        if keep is not None:
            keep[0][row(t), :] = shorted[1]
            keep[1][row(t), :] = shorted[2]
        return carry

    lax.fori_loop(0, tokens + margin, step, 0, unroll=4)


def main_block(
    tokens, margin, modes, part, cols, base, taps, rate, weight, carry_of,
    dq, dk, dv, put_sum, put_tap,
    wide, gated, grad_mixed, keys, values, mixed, grad_gated, trail, outs,
):
    zero = jnp.zeros((GROUPS, LANES), F32)
    for first in range(0, modes, part):
        some = range(first, first + part)
        decay = [jnp.exp(-rate[n, cols, :]) for n in some]
        amount = [weight[n, cols, :] for n in some]

        def total_of(terms):
            terms = list(terms)
            while len(terms) > 1:
                terms = [a + b for a, b in zip(terms[::2], terms[1::2])]
            return terms[0]

        def forward(t, carry):
            x, dots = carry
            u = gated[row(t), :]
            g = grad_mixed[row(t), :]
            x = tuple(decay[n] * x[n] + u for n in range(part))
            for n in range(part):
                trail[row(t * part + n), :] = x[n]
            y = total_of(amount[n] * x[n] for n in range(part))
            if first > 0:
                y = y + mixed[row(t), :]
            mixed[row(t), :] = y
            return (x, tuple(dots[n] + g * x[n] for n in range(part)))

        start = tuple(carry_of(n, 0) for n in some)
        x, dots = lax.fori_loop(0, tokens, forward, (start, (zero,) * part), unroll=4)
        for n in range(part):
            put_sum(0, first + n, dots[n])
        for t in range(tokens, tokens + margin):
            u = gated[row(t), :]
            x = tuple(decay[n] * x[n] + u for n in range(part))
            y = total_of(amount[n] * x[n] for n in range(part))
            if first > 0:
                y = y + mixed[row(t), :]
            mixed[row(t), :] = y

        def backward(i, carry):
            t = tokens - 1 - i
            h, dots = carry
            g = grad_mixed[row(t), :]
            dots = tuple(dots[n] + trail[row(t * part + n), :] * h[n] for n in range(part))
            h = tuple(decay[n] * h[n] + g for n in range(part))
            y = total_of(amount[n] * h[n] for n in range(part))
            if first > 0:
                y = y + grad_gated[row(t), :]
            grad_gated[row(t), :] = y
            return (h, dots)

        start = tuple(carry_of(n, 1) for n in some)
        h, dots = lax.fori_loop(0, tokens, backward, (start, (zero,) * part), unroll=4)
        for n in range(part):
            put_sum(1, first + n, decay[n] * dots[n])
        grow = [jnp.exp(rate[n, cols, :]) for n in some]
        h = start
        for t in range(tokens, tokens + margin):
            y = total_of(amount[n] * h[n] for n in range(part))
            if first > 0:
                y = y + grad_gated[row(t), :]
            grad_gated[row(t), :] = y
            g = grad_mixed[row(t), :]
            h = tuple((h[n] - g) * grow[n] for n in range(part))

    filters = [[taps[i, j, cols, :] for j in range(margin + 1)] for i in range(3)]

    def grads_at(t):
        m = rounded(mixed[row(t), :])
        gg = rounded(grad_gated[row(t), :])
        return (wide[3][row(t + margin), :] * m, gg * values[row(t), :], gg * keys[row(t), :])

    def finish(i, carry):
        t = tokens - 1 - i
        later, dots = carry
        now = grads_at(t)
        window = (now,) + later
        new = []
        for a in range(3):
            total = filters[a][0] * now[a]
            for j in range(1, margin + 1):
                total = total + filters[a][j] * window[j][a]
            outs[a][row(t), :] = total
            for j in range(margin + 1):
                new.append(dots[a * (margin + 1) + j] + now[a] * wide[a][row(t + margin - j), :])
        return (window[:margin], tuple(new))

    later = tuple(grads_at(tokens + j) for j in range(margin))
    later, dots = lax.fori_loop(0, tokens, finish, (later, (zero,) * (3 * (margin + 1))), unroll=4)
    for a in range(3):
        for j in range(margin + 1):
            put_tap(a * (margin + 1) + j, dots[a * (margin + 1) + j])
    for source, target in zip(outs, (dq, dk, dv)):
        gather_rows(source, target, tokens, base)


MESH = pl.DeviceIdType.MESH


def partner(d):
    count = lax.axis_size("seq")
    return lax.rem(lax.axis_index("seq") + d, count)


def core_of():
    return lax.rem(lax.axis_index("dp"), 2)


def other_core():
    return lax.axis_index("dp") + 1 - 2 * core_of()


def same_core(d):
    return lax.rem(lax.axis_index("dp") + 2 * d, lax.axis_size("dp"))


def greet():
    count = lax.axis_size("seq")
    barrier = pltpu.get_barrier_semaphore()

    def step(d, carry):
        pl.semaphore_signal(barrier, inc=1, device_id={"seq": partner(d)}, device_id_type=MESH)
        return carry

    lax.fori_loop(1, count, step, 0)
    pl.semaphore_signal(barrier, inc=1, device_id={"dp": other_core()}, device_id_type=MESH)
    chips = lax.axis_size("dp") // 2
    for d in range(1, chips):
        pl.semaphore_signal(barrier, inc=1, device_id={"dp": same_core(d)}, device_id_type=MESH)
    pl.semaphore_wait(barrier, count + chips - 1)


def remote(source, target, sems, d, device):
    return pltpu.make_async_remote_copy(
        src_ref=source,
        dst_ref=target,
        send_sem=sems.at[0, d],
        recv_sem=sems.at[1, d],
        device_id=device,
        device_id_type=MESH,
    )


class ToAll:

    def __init__(self, source_of, target, sems):
        self.source_of, self.target, self.sems = source_of, target, sems

    def copy(self, d):
        p = partner(d)
        slot = self.target.at[lax.axis_index("seq")]
        return remote(self.source_of(p), slot, self.sems, d, {"seq": p})

    def start(self):
        def step(d, carry):
            self.copy(d).start()
            return carry

        lax.fori_loop(1, lax.axis_size("seq"), step, 0)

    def wait(self):
        def step(d, carry):
            self.copy(d).wait()
            return carry

        lax.fori_loop(1, lax.axis_size("seq"), step, 0)


def to_other_core(ref, sems, d):
    return remote(ref, ref, sems, d, {"dp": other_core()})


class Level:

    def __init__(self, size, mine, device_of, source_of, target, sems):
        self.size, self.mine, self.device_of = size, mine, device_of
        self.source_of, self.target, self.sems = source_of, target, sems

    def copies(self):
        for d in range(1, self.size):
            j = lax.rem(self.mine + d, self.size)
            device = self.device_of(j)
            yield remote(self.source_of(j), self.target.at[self.mine], self.sems, d, device)

    def start(self):
        for copy in self.copies():
            copy.start()

    def wait(self):
        for copy in self.copies():
            copy.wait()


def mixer_kernel(
    tokens, margin, modes, blocks, own, inner, scale,
    q, k, v, c, mine, taps,
    dq, dk, dv, sums, tap_sums,
    w0, w1, w2, w3, gated, grad_mixed, keys, values, mixed, grad_gated, trail, o0, o1, o2,
    slots, table, before, after, left, right, state, got, total, planes, sent, landed,
    packed, other, summed, near_got, near_sum, far_got, chip_got, both, shared,
    slot_sems, halo_sems, swap_sems, out_sems, plane_sems, back_sems,
    add_sems, near_sems, far_sems, chip_sems, share_sems,
):
    me = lax.axis_index("seq")
    count = lax.axis_size("seq")
    core = core_of()
    outer = count // inner
    per = modes // inner
    low = lax.rem(me, inner)
    high = lax.div(me, inner)
    wide = (w0, w1, w2, w3)
    zero = jnp.zeros((GROUPS, LANES), F32)
    per_block = outer // blocks
    chips = lax.axis_size("dp") // 2
    sum_rows = modes * own
    tap_count = 3 * (margin + 1)
    first_taps = (tap_count + 1) // 2
    greet()
    gathers = [
        ToAll(lambda p, i=i: mine.at[i, core], slots.at[i, core], slot_sems.at[i]) for i in range(2)
    ]
    gathers[0].start()
    for i in range(2):
        slots[i, core, me] = mine[i, core]
    for b in range(blocks):
        cols = slice(b * GROUPS, (b + 1) * GROUPS)
        for i, x in enumerate((q, k, v, c)):
            spread_rows(x, wide[i].at[b], margin, tokens, b * WIDE)
            for j in range(margin):
                if i < 3:
                    before[i, j, cols, :] = wide[i][b, row(tokens + j), :]
                after[i, j, cols, :] = wide[i][b, row(margin + j), :]
    halos = [
        remote(before, left, halo_sems, 0, {"seq": partner(1)}),
        remote(after, right, halo_sems, 1, {"seq": partner(count - 1)}),
    ]
    for copy in halos:
        copy.start()
    for halo in halos:
        halo.wait()
    for b in range(blocks):
        cols = slice(b * GROUPS, (b + 1) * GROUPS)
        for i in range(4):
            for j in range(margin):
                if i < 3:
                    wide[i][b, row(j), :] = jnp.where(me > 0, left[i, j, cols, :], 0.0)
                wide[i][b, row(margin + tokens + j), :] = jnp.where(
                    me < count - 1, right[i, j, cols, :], 0.0
                )
    for b in range(blocks):
        short_products(
            tokens, margin, taps[:, :, b * GROUPS : (b + 1) * GROUPS, :],
            [x.at[b] for x in wide], gated.at[b], grad_mixed.at[b], (keys.at[b], values.at[b]),
        )

    def arrange(i):
        copy = to_other_core(slots.at[i, core], swap_sems, 3 * i)
        copy.start()
        copy.wait()
        part = modes // 2

        def step(n, carry):
            for side in range(2):
                for p in range(count):
                    piece = slots[i, side, p, n]
                    table[i, side * part + n, p * own : (p + 1) * own, :] = piece
            return carry

        lax.fori_loop(0, part, step, 0)

    gathers[0].wait()
    gathers[1].start()
    arrange(0)
    rate, weight = table.at[0], table.at[1]

    def near(source, target, sems, b):
        return Level(
            inner, low, lambda j: {"seq": high * inner + j}, lambda j: source.at[b, j], target.at[b], sems.at[b]
        )

    def far(b):
        def source_of(j):
            return total.at[b, jnp.where(j > high, 0, 1)]

        return Level(
            outer, high, lambda j: {"seq": j * inner + low}, source_of, planes.at[b], plane_sems.at[b]
        )

    def power(n, cols, times):
        return jnp.exp(-times * tokens * table[0, low * per + n, cols, :])

    def add_group(b):
        near(state, got, out_sems, b).wait()
        cols = slice(b * GROUPS, (b + 1) * GROUPS)
        for n in range(per):
            factor = power(n, cols, 1)
            ahead = got[b, 0, 0, n]
            back = got[b, inner - 1, 1, n]
            for j in range(1, inner):
                ahead = factor * ahead + got[b, j, 0, n]
                back = factor * back + got[b, inner - 1 - j, 1, n]
            total[b, 0, n] = ahead
            total[b, 1, n] = back
        far(b).start()

    def give_back(b):
        far(b).wait()
        cols = slice(b * GROUPS, (b + 1) * GROUPS)
        for n in range(per):
            factor = power(n, cols, 1)
            jump = power(n, cols, inner)
            ahead = lax.fori_loop(0, high, lambda z, x: jump * x + planes[b, z, n], zero)
            back = lax.fori_loop(
                high + 1, outer, lambda z, x: jump * x + planes[b, outer + high - z, n], zero
            )
            for j in range(inner):
                sent[b, j, 0, n] = ahead
                ahead = factor * ahead + got[b, j, 0, n]
                sent[b, inner - 1 - j, 1, n] = back
                back = factor * back + got[b, inner - 1 - j, 1, n]
        near(sent, landed, back_sems, b).start()
        landed[b, low] = sent[b, low]

    packed[...] = jnp.zeros_like(packed)

    def put_rows(b, part, start, tile):
        for o in range(per_block * inner):
            target = packed.at[part, b * per_block + o // inner, o % inner]
            target[start : start + own, :] = tile[o * own : (o + 1) * own, :]

    def add_cores(b):
        some = pl.ds(b * per_block, per_block)
        return remote(
            packed.at[1 - core, some], other.at[some], add_sems, b, {"dp": other_core()}
        )

    def near_sums(z):
        return Level(
            inner, low, lambda j: {"seq": high * inner + j},
            lambda j: summed.at[z, j], near_got.at[z], near_sems.at[z],
        )

    far_sums = Level(
        outer, high, lambda j: {"seq": j * inner + low}, lambda j: near_sum.at[j], far_got, far_sems
    )

    def pass_near(b):
        add_cores(b).wait()
        for z in range(b * per_block, (b + 1) * per_block):
            summed[z] = packed[core, z] + other[z]
            near_sums(z).start()
            near_got[z, low] = summed[z, low]

    def pass_far(b):
        for z in range(b * per_block, (b + 1) * per_block):
            near_sums(z).wait()
            terms = near_got[z, 0]
            for j in range(1, inner):
                terms = terms + near_got[z, j]
            near_sum[z] = terms

            @pl.when(high == z)
            def _():
                far_got[z] = terms

            @pl.when(high != z)
            def _():
                d = lax.rem(z - high + outer, outer)
                device = {"seq": z * inner + low}
                remote(near_sum.at[z], far_got.at[high], far_sems, d, device).start()

    for b in range(blocks):
        cols = slice(b * GROUPS, (b + 1) * GROUPS)
        u_ref, g_ref = gated.at[b], grad_mixed.at[b]
        decay = [jnp.exp(-rate[n, cols, :]) for n in range(modes)]

        def step(t, carry):
            ahead, back = carry
            u = u_ref[row(t), :]
            g = g_ref[row(tokens - 1 - t), :]
            return (
                tuple(decay[n] * ahead[n] + u for n in range(modes)),
                tuple(decay[n] * back[n] + g for n in range(modes)),
            )

        ends = lax.fori_loop(0, tokens, step, ((zero,) * modes, (zero,) * modes), unroll=4)
        for n in range(modes):
            for i in range(2):
                state[b, n // per, i, n % per] = ends[i][n]
        near(state, got, out_sems, b).start()
        got[b, low] = state[b, low]
        if b > 0:
            add_group(b - 1)
        if b > 1:
            give_back(b - 2)
    add_group(blocks - 1)
    if blocks > 1:
        give_back(blocks - 2)
    gathers[1].wait()
    arrange(1)
    for b in range(blocks):
        if blocks == 1:
            give_back(b)
        near(sent, landed, back_sems, b).wait()

        def put_sum(i, n, tile):
            put_rows(b, i, n * own, tile)

        def put_tap(n, tile):
            part, place = (0, n) if n < first_taps else (1, n - first_taps)
            put_rows(b, part, sum_rows + place * own, tile)

        main_block(
            tokens, margin, modes, modes // 2, slice(b * GROUPS, (b + 1) * GROUPS), b * WIDE,
            taps, rate, weight, lambda n, i: landed[b, n // per, i, n % per],
            dq, dk, dv, put_sum, put_tap,
            [x.at[b] for x in wide], gated.at[b], grad_mixed.at[b], keys.at[b], values.at[b],
            mixed, grad_gated, trail, (o0, o1, o2),
        )
        if b == 0 and blocks > 1:
            give_back(blocks - 1)
        add_cores(b).start()
        if b > 0:
            pass_near(b - 1)
        if b > 1:
            pass_far(b - 2)
    pass_near(blocks - 1)
    if blocks > 1:
        pass_far(blocks - 2)
    pass_far(blocks - 1)
    far_sums.wait()
    total_rows = far_got[0]
    for z in range(1, outer):
        total_rows = total_rows + far_got[z]
    if chips > 1:
        chip = lax.div(lax.axis_index("dp"), 2)
        chip_got[chip] = total_rows
        level = Level(
            chips, chip, lambda j: {"dp": 2 * j + core},
            lambda j: chip_got.at[chip], chip_got, chip_sems,
        )
        level.start()
        level.wait()
        total_rows = chip_got[0]
        for z in range(1, chips):
            total_rows = total_rows + chip_got[z]
    total_rows = total_rows * scale
    shared[core, me] = total_rows[sum_rows:]
    sharing = ToAll(lambda p: shared.at[core, me], shared.at[core], share_sems)
    sharing.start()
    both[core] = total_rows[:sum_rows]
    swap_sums = to_other_core(both.at[core], swap_sems, 1)
    swap_sums.start()
    sharing.wait()
    swap_taps = to_other_core(shared.at[core], swap_sems, 2)
    swap_taps.start()
    swap_sums.wait()
    sums[...] = both[...]
    swap_taps.wait()
    for n in range(tap_count):
        part, place = (0, n) if n < first_taps else (1, n - first_taps)
        for p in range(count):
            tap_sums[n, p * own : (p + 1) * own, :] = shared[
                part, p, place * own : (place + 1) * own, :
            ]


def comm_call(kernel, ident, name, shapes, scratch):
    return pl.pallas_call(
        kernel,
        out_shape=shapes,
        scratch_shapes=scratch,
        compiler_params=pltpu.CompilerParams(
            collective_id=ident, has_side_effects=True, vmem_limit_bytes=56 << 20
        ),
        name=name,
    )


def body(query_rows, key_rows, value_rows, cotangent, short_filter, residue, decay_rate):
    batch, tokens, width = query_rows.shape
    assert batch == 1
    margin = short_filter.shape[1] - 1
    modes = residue.shape[1]
    count = lax.axis_size("seq")
    own = residue.shape[0] // LANES
    tiles = width // LANES
    blocks = width // WIDE
    inner = 4
    assert count % inner == 0 and modes % inner == 0
    outer, per = count // inner, modes // inner
    length = tokens * count

    root = jnp.sqrt(-jnp.expm1(-2.0 * decay_rate))
    each = pltpu.SemaphoreType.DMA((2, count))
    few = pltpu.SemaphoreType.DMA((2, 4))
    each_twice = pltpu.SemaphoreType.DMA((2, 2, count))
    cores = lax.axis_size("dp")
    scale = 1.0 / math.sqrt(batch * cores * length)
    tap_count = 3 * (margin + 1)
    tap_rows = -(-((tap_count + 1) // 2 * own) // 8) * 8
    rows_each = modes * own + tap_rows
    mine = jnp.stack([decay_rate.T, (residue * root).T]).reshape(2, 2, modes // 2, own, LANES)
    rows = (query_rows, key_rows, value_rows, cotangent)
    taps = short_filter.reshape(3, margin + 1, tiles, LANES)

    def scratch(n, *lead):
        return pltpu.VMEM(lead + (n * GROUPS, LANES), F32)

    def vmem_like(shape):
        return pltpu.VMEM(shape, F32)

    group = (blocks, inner, 2, per, GROUPS, LANES)
    levels = pltpu.SemaphoreType.DMA((blocks, 2, inner))
    far_level = pltpu.SemaphoreType.DMA((blocks, 2, outer))
    halo = [vmem_like((i, margin, tiles, LANES)) for i in (3, 4)]
    dq, dk, dv, sums, tap_sums = comm_call(
        functools.partial(mixer_kernel, tokens, margin, modes, blocks, own, inner, scale),
        0,
        "mixer",
        [jax.ShapeDtypeStruct(query_rows.shape, BF16)] * 3
        + [
            jax.ShapeDtypeStruct((2, modes * own, LANES), F32),
            jax.ShapeDtypeStruct((tap_count, tiles, LANES), F32),
        ],
        [scratch(tokens + 2 * margin, blocks)] * 4
        + [scratch(tokens + margin, blocks)] * 4
        + [scratch(tokens + margin)] * 2
        + [scratch(tokens * modes // 2)]
        + [scratch(tokens)] * 3
        + [vmem_like((2, 2, count, modes // 2, own, LANES)), vmem_like((2, modes, tiles, LANES))]
        + halo * 2
        + [vmem_like(group)] * 2
        + [
            vmem_like((blocks, 2, per, GROUPS, LANES)),
            vmem_like((blocks, outer, per, GROUPS, LANES)),
        ]
        + [vmem_like(group)] * 2
        + [
            vmem_like((2, outer, inner, rows_each, LANES)),
            vmem_like((outer, inner, rows_each, LANES)),
            vmem_like((outer, inner, rows_each, LANES)),
            vmem_like((outer, inner, rows_each, LANES)),
            vmem_like((outer, rows_each, LANES)),
            vmem_like((outer, rows_each, LANES)),
            vmem_like((max(cores // 2, 1), rows_each, LANES)),
            vmem_like((2, modes * own, LANES)),
            vmem_like((2, count, tap_rows, LANES)),
        ]
        + [each_twice, few, few, levels, far_level, levels]
        + [
            pltpu.SemaphoreType.DMA((2, blocks)),
            pltpu.SemaphoreType.DMA((outer, 2, inner)),
            pltpu.SemaphoreType.DMA((2, outer)),
            pltpu.SemaphoreType.DMA((2, max(cores // 2, 1))),
            each,
        ],
    )(*rows, mine, taps)

    filter_grad = tap_sums.reshape(3, margin + 1, width)
    first_sum, second_sum = (
        sums.reshape(2, modes, own * LANES).transpose(0, 2, 1)
    )
    residue_grad = root * first_sum
    rate_grad = (
        residue * jnp.exp(-2.0 * decay_rate) / root * first_sum - residue * root * second_sum
    )
    return (dq, dk, dv, filter_grad, residue_grad, decay_rate * rate_grad)


def solution(mesh):
    rows = P("dp", "seq", None)
    modes = P("seq", None)
    return jax.shard_map(
        body,
        mesh=mesh,
        in_specs=(rows, rows, rows, rows, P(), modes, modes),
        out_specs=(rows, rows, rows, P(), modes, modes),
        check_vma=False,
    )
```
